32 devices in a mesh: groups: 2 (over y), tensor: 4 (over z), batch: 2 (over x), rep: 2 (over core).
Axes of the slice: x: 2, y: 2, z: 4, core: 2. Of those that a mesh axis runs over, the one named last changes fastest.
Arguments:
- ri_tensor: bfloat16 [64, 64, 4096], P(('groups', 'tensor')), parts along dimension 0, may hold values from -0.29882812 to 0.29882812
- pair_ids: int32 [512], P(('groups', 'tensor')), parts along dimension 0, may hold values from 0 to 255, as said below
- atom_size: int32 [16], replicated, may hold values from 32 to 64
- green_occ: bfloat16 [1024, 1024], replicated, may hold values from -0.1875 to 0.1875
- green_virt: bfloat16 [1024, 1024], P(None, ('batch', 'rep')), may hold values from -0.375 to 0.375
Outputs:
- response: float32 [64, 32], P(('groups', 'tensor'), ('batch', 'rep')), parts along dimension 0
The draws below stay inside these ranges and needn't reach their ends.
There are 2 independent parts, one for each index of `groups`. The reference program is written for one: setup_inputs(seed, part) draws one part's arguments, and reference() takes and returns one part's arrays. A program takes and returns all parts, laid end to end along the dimension named above; an argument that names none is the same for every part. Nothing has to cross between parts.
Inputs may be any that keep to these rules, and one draw needn't show every extreme that they name: `pair_ids`: entry e names the atom pair (e // 16, e % 16); the 64 entries of one tensor index are distinct.
All inputs are finite; a program needn't handle non-finite values.
Results may differ from the reference program's by a relative error of at most 0.012.
Values may be sent and summed in bfloat16 or wider, within the bound.
A program may use at most 192 MiB of HBM per device.

```python
import jax
import jax.numpy as jnp
from jax import lax

NAT = 16
BS = 64
SLOTS = 64
PT = 8
NAO = 1024
RI = 32
PAIRS = 256


def draw_pair_ids(key, part):
    key = jax.random.fold_in(key, 7)

    def one_index(index):
        return jax.random.permutation(jax.random.fold_in(key, index), NAT * NAT)[:SLOTS]
    return jax.vmap(one_index)(jnp.arange(PAIRS // SLOTS)).reshape(PAIRS).astype(jnp.int32)


def place_ends(result, own_key, smallest, high):
    place = [jax.random.randint(jax.random.fold_in(own_key, axis), (), 0, length) for axis, length in enumerate(result.shape)]
    main_axis = result.shape.index(max(result.shape))
    neighbour = place[:main_axis] + [(place[main_axis] + 1) % result.shape[main_axis]] + place[main_axis + 1:]
    return result.at[tuple(place)].set(smallest).at[tuple(neighbour)].set(high)


def level_of(own_key, extent, cuts, low, largest):
    def one(position, parts):
        steps = jax.random.uniform(jax.random.fold_in(jax.random.fold_in(own_key, 6), position), (parts,), jnp.float32, low / len(cuts), largest / len(cuts))
        return jnp.repeat(jnp.exp(steps), extent[position] // parts).reshape((-1,) + (1,) * (len(extent) - position - 1))

    loudness = one(*cuts[0])
    for cut in cuts[1:]:
        loudness = loudness * one(*cut)
    return loudness


def centred(stream_key, dims, scale, limit, shards=(), held_as=jnp.bfloat16):
    level = level_of(stream_key, dims, shards, -0.22, 0.18) if shards else 1.0
    array = jax.random.normal(stream_key, dims, jnp.float32) * scale * level
    return jnp.minimum(jnp.maximum(array, -limit), limit).astype(held_as)


def setup_inputs(seed: int = 0, part: int = 0) -> dict:
    keys = jax.random.split(jax.random.key(seed), 6)
    part_splits = jax.random.split(jax.random.fold_in(keys[5], part), 6)
    ri_tensor = centred(part_splits[0], (RI, SLOTS, BS * BS), 0.05, 0.29882812, ((0, 4),))
    pair_ids = draw_pair_ids(jax.random.fold_in(jax.random.fold_in(keys[5], part), 71), part)
    atom_size = place_ends(jax.random.randint(keys[2], (NAT,), BS // 2, BS + 1), jax.random.fold_in(keys[2], 1), BS // 2, BS).astype(jnp.int32)
    green_occ = centred(keys[3], (NAO, NAO), NAO ** -0.5, 0.1875)
    green_virt = centred(keys[4], (NAO, NAO), (SLOTS * BS // NAT) ** -0.5, 0.375, ((1, 4),))
    return {"ri_tensor": ri_tensor, "pair_ids": pair_ids, "atom_size": atom_size, "green_occ": green_occ, "green_virt": green_virt}


def reference(ri_tensor, pair_ids, atom_size, green_occ, green_virt):
    usable = (jnp.arange(BS)[None, :] < atom_size[:, None]).astype(jnp.float32).reshape(NAO)
    mask_full = (usable[:, None] * usable[None, :]).astype(jnp.bfloat16)

    def one_index(index):
        start = (index * PT).astype(jnp.int32)
        blocks = lax.dynamic_slice_in_dim(ri_tensor, start, PT, 0).reshape(PT, SLOTS, BS, BS)
        listed = lax.dynamic_slice_in_dim(pair_ids, (index * SLOTS).astype(jnp.int32), SLOTS, 0)
        panel = jnp.zeros((PT, NAT * NAT, BS, BS), jnp.bfloat16).at[:, listed].set(blocks)
        panel = panel.reshape(PT, NAT, NAT, BS, BS).transpose(0, 1, 3, 2, 4).reshape(PT, NAO, NAO)
        panel = panel * mask_full
        virt_side = jnp.einsum("pmn,ns->pms", panel.astype(jnp.float32), green_virt.astype(jnp.float32),
                               precision=lax.Precision.HIGHEST).astype(jnp.bfloat16)
        occ_side = jnp.einsum("lm,pms->pls", green_occ.astype(jnp.float32), virt_side.astype(jnp.float32),
                              precision=lax.Precision.HIGHEST).astype(jnp.bfloat16)
        return occ_side, panel

    occ_all, tensor_all = lax.map(one_index, jnp.arange(RI // PT, dtype=jnp.int32))
    occ_all = occ_all.reshape(RI, NAO * NAO)
    tensor_all = tensor_all.reshape(RI, NAO * NAO)
    return jnp.dot(occ_all, tensor_all.T, preferred_element_type=jnp.float32)
```

```python
import functools

import jax
import jax.numpy as jnp
from jax import lax
from jax.experimental import pallas as pl
from jax.experimental.pallas import tpu as pltpu
from jax.sharding import PartitionSpec as P

NAT = 16
BS = 64
MESH = pl.DeviceIdType.MESH
NT = (((1,), (1,)), ((), ()))


def gather_kernel(nz, ri, ids_k, ids_n, size, go, gv, out,
                  slabs, perm, tmp, gop, gvm, sel, dense, virt, flat, idbuf, part, parts,
                  zsend, zrecv, xsend, xrecv, csend, crecv, isend, irecv, psend, precv, lsem):
    z = lax.axis_index("tensor")
    b = lax.axis_index("batch")
    r = lax.axis_index("rep")
    j = b * 2 + r
    pieces = 4
    waves = (nz - 1) * pieces
    left = {"tensor": z - 1}
    right = {"tensor": z + 1}
    across = {"batch": 1 - b}
    mate = {"rep": 1 - r}
    diag = {"batch": 1 - b, "rep": 1 - r}

    barrier = pltpu.get_barrier_semaphore()
    for step in range(1, nz):
        pl.semaphore_signal(barrier, inc=1, device_id={"tensor": lax.rem(z + step, nz)}, device_id_type=MESH)
    for dev in (across, mate, diag):
        pl.semaphore_signal(barrier, inc=1, device_id=dev, device_id_type=MESH)

    def local(q):
        return pltpu.make_async_copy(
            ri.at[:, pl.ds(16 * q, 16), :],
            slabs.at[z, q], lsem.at[q])

    def remote(src, dst, s, d, dev):
        return pltpu.make_async_remote_copy(src_ref=src, dst_ref=dst, send_sem=s, recv_sem=d,
                                            device_id=dev, device_id_type=MESH)

    def spot(o, p, q):
        return slabs.at[o, q, pl.ds(2 * p, 2)]

    for q in range(4):
        local(q).start()
    pl.semaphore_wait(barrier, nz - 1 + 3)

    def own(p, d):
        src = ri.at[pl.ds(2 * p, 2), pl.ds(pl.multiple_of(16 * j, 16), 16), :]
        return remote(src, spot(z, p, j), zsend.at[d, p], zrecv.at[d, p], right if d == 0 else left)

    def ids_copy(step):
        dev = {"tensor": lax.rem(z + step, nz)}
        return remote(ids_n, idbuf.at[z], isend.at[step], irecv.at[step], dev)

    for step in range(1, nz):
        ids_copy(step).start()
    for p in range(pieces):
        @pl.when(z < nz - 1)
        def _():
            own(p, 0).start()

        @pl.when(z > 0)
        def _():
            own(p, 1).start()

    def origin(d, t):
        return z - 1 - t if d == 0 else z + 1 + t

    def here(d, t):
        return t <= z - 1 if d == 0 else t <= nz - 2 - z

    def passes(d, t):
        ok = here(d, t)
        return jnp.logical_and(ok, z < nz - 1) if d == 0 else jnp.logical_and(ok, z > 0)

    def z_copy(d, w, o, p):
        return remote(spot(o, p, j), spot(o, p, j), zsend.at[d, w + pieces], zrecv.at[d, w + pieces],
                      right if d == 0 else left)

    def z_in(d, w, o, p):
        return remote(spot(o, p, j), spot(o, p, j), zsend.at[d, w], zrecv.at[d, w], right if d == 0 else left)

    def x_copy(d, w, o, p, q):
        return remote(spot(o, p, q), spot(o, p, q), xsend.at[d, w], xrecv.at[d, w], across)

    def c_copy(d, w, k, o, p, q):
        return remote(spot(o, p, q), spot(o, p, q), csend.at[d, w, k], crecv.at[d, w, k], mate)

    jx = (1 - b) * 2 + r
    jm = b * 2 + 1 - r
    jd = (1 - b) * 2 + 1 - r

    def arrive(w):
        t, p = w // pieces, w % pieces
        for d in (0, 1):
            @pl.when(here(d, t))
            def _():
                o = origin(d, t)
                z_in(d, w, o, p).wait_recv()

                @pl.when(passes(d, t))
                def _():
                    z_copy(d, w, o, p).start()
                x_copy(d, w, o, p, j).start()
                c_copy(d, w, 0, o, p, j).start()

    def spread(w):
        t, p = w // pieces, w % pieces
        for d in (0, 1):
            @pl.when(here(d, t))
            def _():
                o = origin(d, t)
                x_copy(d, w, o, p, jx).wait_recv()
                c_copy(d, w, 1, o, p, jx).start()

    def collect(w):
        t, p = w // pieces, w % pieces
        for d in (0, 1):
            @pl.when(here(d, t))
            def _():
                o = origin(d, t)
                c_copy(d, w, 0, o, p, jm).wait_recv()
                c_copy(d, w, 1, o, p, jd).wait_recv()

    lane = lax.broadcasted_iota(jnp.int32, (1, 1024), 1)
    limit = jnp.zeros((1, 1024), jnp.int32)
    for a in range(16):
        limit = jnp.where(lane // 64 == a, size[a], limit)

    def build(k, _):
        row = lax.broadcasted_iota(jnp.int32, (128, 1024), 0) + k * 128
        col = lax.broadcasted_iota(jnp.int32, (128, 1024), 1)
        place = (col % 64) * 16 + col // 64
        keep = jnp.logical_and(place == row, col % 64 < limit)
        perm[pl.ds(pl.multiple_of(k * 128, 128), 128), :] = jnp.where(keep, 1.0, 0.0).astype(jnp.bfloat16)
        return 0

    lax.fori_loop(0, 8, build, 0)

    def rows_in(k, _):
        at = pl.ds(pl.multiple_of(k * 256, 256), 256)
        tmp[at, :] = jnp.dot(perm[at, :], go[...], preferred_element_type=jnp.float32).astype(jnp.bfloat16)
        return 0

    lax.fori_loop(0, 4, rows_in, 0)

    def cols_in(k, _):
        at = pl.ds(pl.multiple_of(k * 256, 256), 256)
        gop[at, :] = lax.dot_general(tmp[at, :], perm[...], NT,
                                     preferred_element_type=jnp.float32).astype(jnp.bfloat16)
        return 0

    lax.fori_loop(0, 4, cols_in, 0)

    lane256 = lax.broadcasted_iota(jnp.int32, (64, 256), 1)
    sub256 = lax.broadcasted_iota(jnp.int32, (64, 256), 0)
    limit_c = jnp.zeros((64, 256), jnp.int32)
    for c in range(4):
        limit_c = jnp.where(lane256 // 64 == c, size[j * 4 + c], limit_c)
    for c in range(16):
        keep = jnp.logical_and(sub256 < size[c], lane256 % 64 < limit_c)
        block = gv[c * 64:(c + 1) * 64, :].astype(jnp.float32)
        gvm[c * 64:(c + 1) * 64, :] = jnp.where(keep, block, 0.0).astype(jnp.bfloat16)

    row = lax.broadcasted_iota(jnp.int32, (256, 64), 0)
    want = (row % 16) * 16 + ((row % 128) // 16) * 2 + row // 128
    sel[...] = jnp.where(ids_k[...] == want, 1.0, 0.0).astype(jnp.bfloat16)
    idbuf[z] = ids_n[...]
    part[...] = jnp.zeros_like(part)
    for q in range(4):
        local(q).wait()

    low = lax.broadcasted_iota(jnp.int32, (128, 128), 1) < 64
    low16 = lax.broadcasted_iota(jnp.int32, (32, 128), 1) < 64

    def one_function(f):
        def unpack(k, _):
            at = pl.ds(pl.multiple_of(k * 256, 256), 256)
            mine = jnp.concatenate([slabs[z, q, f, :, at] for q in range(4)], axis=0)
            got = jnp.dot(sel[...], mine, preferred_element_type=jnp.float32)
            for h in range(2):
                even, odd = got[:128, h * 128:(h + 1) * 128], got[128:, h * 128:(h + 1) * 128]
                first = jnp.where(low, even, pltpu.roll(odd, 64, 1)).astype(jnp.bfloat16)
                second = jnp.where(low, pltpu.roll(even, 64, 1), odd).astype(jnp.bfloat16)
                base = k * 64 + h * 32
                for c in range(8):
                    dense[pl.ds(pl.multiple_of(base, 16), 16), c * 128:(c + 1) * 128] = first[c * 16:(c + 1) * 16]
                    dense[pl.ds(pl.multiple_of(base + 16, 16), 16), c * 128:(c + 1) * 128] = second[c * 16:(c + 1) * 16]
            return 0

        lax.fori_loop(0, 16, unpack, 0)

        def virt_step(k, _):
            at = pl.ds(pl.multiple_of(k * 256, 256), 256)
            virt[at, :] = jnp.dot(dense[at, :], gvm[...], preferred_element_type=jnp.float32).astype(jnp.bfloat16)
            return 0

        lax.fori_loop(0, 4, virt_step, 0)

        def occ_step(k, _):
            at = pl.ds(pl.multiple_of(k * 256, 256), 256)
            occ = jnp.dot(gop[at, :], virt[...], preferred_element_type=jnp.float32)
            for h in range(8):
                even, odd = occ[h * 32:h * 32 + 16], occ[h * 32 + 16:h * 32 + 32]
                even = jnp.concatenate([even[:, :128], even[:, 128:]], axis=0)
                odd = jnp.concatenate([odd[:, :128], odd[:, 128:]], axis=0)
                first = jnp.where(low16, even, pltpu.roll(odd, 64, 1)).astype(jnp.bfloat16)
                second = jnp.where(low16, pltpu.roll(even, 64, 1), odd).astype(jnp.bfloat16)
                lanes = pl.ds(pl.multiple_of(k * 1024 + h * 128, 128), 128)
                flat[pl.ds(pl.multiple_of(f * 64, 32), 32), lanes] = first
                flat[pl.ds(pl.multiple_of(f * 64 + 32, 32), 32), lanes] = second
            return 0

        lax.fori_loop(0, 4, occ_step, 0)

    row64 = lax.broadcasted_iota(jnp.int32, (64, 128), 0)
    want64 = (row64 % 16) * 16 + j * 4 + ((row64 % 32) // 16) * 2 + row64 // 32
    out_lane = lax.broadcasted_iota(jnp.int32, (8, 128), 1)

    def contract(o, p):
        other = jnp.concatenate([slabs[o, q, pl.ds(2 * p, 2)].reshape(32, 4096) for q in range(4)], axis=0)
        pick = idbuf[o] == want64
        halves = jnp.zeros((8, 128), jnp.float32)
        for m in range(2):
            gram = lax.dot_general(flat[m * 256:(m + 1) * 256, :], other, NT, preferred_element_type=jnp.float32)
            for f in range(4):
                kept = jnp.sum(jnp.where(pick, gram[f * 64:(f + 1) * 64], 0.0), axis=0, keepdims=True)
                halves = jnp.where(lax.broadcasted_iota(jnp.int32, (8, 128), 0) == m * 4 + f, kept, halves)
        add = jnp.zeros((8, 128), jnp.float32)
        for q in range(2):
            total = jnp.sum(jnp.where((out_lane // 16) % 2 == q, halves, 0.0), axis=1, keepdims=True)
            add = add + jnp.where(out_lane == o * 8 + p * 2 + q, total, 0.0)
        part[...] += add

    def contract_wave(w):
        t, p = w // pieces, w % pieces
        for d in (0, 1):
            @pl.when(here(d, t))
            def _():
                contract(origin(d, t), p)

    def first_phase(w, _):
        one_function(2 * w)
        arrive(w)

        @pl.when(w > 0)
        def _():
            spread(w - 1)
        one_function(2 * w + 1)
        return 0

    lax.fori_loop(0, 4, first_phase, 0)
    for step in range(1, nz):
        ids_copy(step).wait_send()
        remote(ids_n, idbuf.at[z], isend.at[step], irecv.at[step], right).wait_recv()

    def own_slab(p, _):
        contract(z, p)
        return 0

    arrive(4)
    spread(3)
    lax.fori_loop(0, 2, own_slab, 0)
    arrive(5)
    spread(4)
    lax.fori_loop(2, 4, own_slab, 0)

    def catch_up(w, _):
        collect(w)
        contract_wave(w)
        return 0

    lax.fori_loop(0, 3, catch_up, 0)

    def second_phase(w, _):
        @pl.when(w < waves)
        def _():
            arrive(w)

        @pl.when(w < waves + 1)
        def _():
            spread(w - 1)
        collect(w - 3)
        contract_wave(w - 3)
        return 0

    lax.fori_loop(6, waves + 3, second_phase, 0)

    def p_copy(k, dev):
        return remote(part, parts.at[k], psend.at[k], precv.at[k], dev)

    for k, dev in enumerate((across, mate, diag)):
        p_copy(k, dev).start()

    def finish(w, _):
        t, p = w // pieces, w % pieces
        for d in (0, 1):
            @pl.when(here(d, t))
            def _():
                o = origin(d, t)

                @pl.when(passes(d, t))
                def _():
                    z_copy(d, w, o, p).wait_send()
                x_copy(d, w, o, p, j).wait_send()
                c_copy(d, w, 0, o, p, j).wait_send()
                c_copy(d, w, 1, o, p, jx).wait_send()
        return 0

    lax.fori_loop(0, waves, finish, 0)
    for p in range(pieces):
        @pl.when(z < nz - 1)
        def _():
            own(p, 0).wait_send()

        @pl.when(z > 0)
        def _():
            own(p, 1).wait_send()
    for k, dev in enumerate((across, mate, diag)):
        p_copy(k, dev).wait()
    total = part[...] + parts[0] + parts[1] + parts[2]
    wide = out.shape[1]
    result = jnp.zeros(out.shape, jnp.float32)
    for q in range(4):
        result = jnp.where(j == q, total[:, q * wide:(q + 1) * wide], result)
    out[...] = result


def fused(nz, ri_tensor, pair_ids, atom_size, green_occ, green_virt):
    ids_n = jnp.broadcast_to(pair_ids.reshape(4, 1, 16), (4, 2, 16)).reshape(1, 128)
    waves = (nz - 1) * 4
    vmem = pl.BlockSpec(memory_space=pltpu.VMEM)
    bf16 = jnp.bfloat16
    dma = pltpu.SemaphoreType.DMA
    return pl.pallas_call(
        functools.partial(gather_kernel, nz),
        out_shape=jax.ShapeDtypeStruct((8, nz * 2), jnp.float32),
        in_specs=[pl.BlockSpec(memory_space=pl.ANY), vmem, vmem,
                  pl.BlockSpec(memory_space=pltpu.SMEM), vmem, vmem],
        out_specs=vmem,
        scratch_shapes=[
            pltpu.VMEM((nz, 4, 8, 16, 4096), bf16),
            pltpu.VMEM((1024, 1024), bf16),
            pltpu.VMEM((1024, 1024), bf16),
            pltpu.VMEM((1024, 1024), bf16),
            pltpu.VMEM((1024, 256), bf16),
            pltpu.VMEM((256, 64), bf16),
            pltpu.VMEM((1024, 1024), bf16),
            pltpu.VMEM((1024, 256), bf16),
            pltpu.VMEM((512, 4096), bf16),
            pltpu.VMEM((nz, 1, 128), jnp.int32),
            pltpu.VMEM((8, 128), jnp.float32),
            pltpu.VMEM((3, 8, 128), jnp.float32),
            dma((2, waves + 4)), dma((2, waves + 4)),
            dma((2, waves)), dma((2, waves)),
            dma((2, waves, 2)), dma((2, waves, 2)),
            dma((nz,)), dma((nz,)), dma((3,)), dma((3,)), dma((4,)),
        ],
        compiler_params=pltpu.CompilerParams(
            collective_id=0, has_side_effects=True, vmem_limit_bytes=56 * 1024 * 1024),
    )(ri_tensor, pair_ids.reshape(1, 64), ids_n, atom_size, green_occ, green_virt)


def per_device(ri_tensor, pair_ids, atom_size, green_occ, green_virt):
    nz = lax.axis_size("tensor")
    split = (lax.axis_size("batch"), lax.axis_size("rep"))
    if nz == 4 and split == (2, 2) and ri_tensor.shape == (8, 64, 4096) and green_occ.shape == (1024, 1024):
        return fused(nz, ri_tensor, pair_ids, atom_size, green_occ, green_virt)
    return whole_blocks(ri_tensor, pair_ids, atom_size, green_occ, green_virt)


def whole_blocks(ri_tensor, pair_ids, atom_size, green_occ, green_virt):
    local_rows = ri_tensor.shape[0]
    slots = ri_tensor.shape[1]
    total_ao = green_occ.shape[0]
    columns = green_virt.shape[1]
    first_col = (lax.axis_index("batch") * lax.axis_size("rep") + lax.axis_index("rep")) * columns
    usable = (jnp.arange(BS)[None, :] < atom_size[:, None]).astype(jnp.bfloat16)
    row_atoms = pair_ids // NAT
    col_atoms = pair_ids % NAT
    blocks = ri_tensor.reshape(local_rows, slots, BS, BS)
    blocks = blocks * usable[row_atoms][None, :, :, None] * usable[col_atoms][None, :, None, :]
    selector_f = row_atoms[None, :] == jnp.arange(NAT)[:, None]
    selector = selector_f.astype(jnp.bfloat16)
    block_cols = col_atoms[:, None] * BS + jnp.arange(BS)[None, :]
    wanted = first_col + jnp.arange(columns)
    picker = (block_cols[:, :, None] == wanted[None, None, :]).astype(jnp.bfloat16)
    picked = jnp.einsum(
        "psij,sjk->psik", blocks, picker, preferred_element_type=jnp.float32
    ).astype(jnp.bfloat16)
    tensor_piece = jnp.einsum("as,psik->paik", selector, picked, preferred_element_type=jnp.float32)
    tensor_piece = tensor_piece.astype(jnp.bfloat16).reshape(local_rows, total_ao, columns)
    gv_blocks = green_virt.reshape(NAT, BS, columns)[col_atoms]
    per_slot = jnp.einsum("psij,sjk->psik", blocks, gv_blocks, preferred_element_type=jnp.float32)
    upper = per_slot.astype(jnp.bfloat16)
    rest = per_slot - upper.astype(jnp.float32)
    middle = rest.astype(jnp.bfloat16)
    lower = (rest - middle.astype(jnp.float32)).astype(jnp.bfloat16)
    virt_side = jnp.einsum("as,psik->paik", selector, upper, preferred_element_type=jnp.float32)
    virt_side = virt_side + jnp.einsum(
        "as,psik->paik", selector, middle, preferred_element_type=jnp.float32
    )
    virt_side = virt_side + jnp.einsum(
        "as,psik->paik", selector, lower, preferred_element_type=jnp.float32
    )
    virt_side = virt_side.astype(jnp.bfloat16).reshape(local_rows, total_ao, columns)
    occ_side = jnp.einsum(
        "lm,pms->pls", green_occ, virt_side, preferred_element_type=jnp.float32
    ).astype(jnp.bfloat16)
    moved_occ, moved_tensor = (
        lax.all_to_all(occ_side, "tensor", split_axis=1, concat_axis=0, tiled=True),
        lax.all_to_all(tensor_piece, "tensor", split_axis=1, concat_axis=0, tiled=True),
    )
    partial_value = jnp.einsum(
        "pls,qls->pq", moved_occ, moved_tensor, preferred_element_type=jnp.float32
    )
    own_rows = lax.psum_scatter(partial_value, "tensor", scatter_dimension=0, tiled=True)
    return lax.psum_scatter(own_rows, ("batch", "rep"), scatter_dimension=1, tiled=True)


def solution(mesh):
    in_specs = (
        P(("groups", "tensor"), None, None),
        P(("groups", "tensor")),
        P(),
        P(),
        P(None, ("batch", "rep")),
    )
    out_specs = P(("groups", "tensor"), ("batch", "rep"))
    return jax.shard_map(
        per_device, mesh=mesh, in_specs=in_specs, out_specs=out_specs, check_vma=False
    )
```

```python
import functools

import jax
import jax.numpy as jnp
from jax import lax
from jax.experimental import pallas as pl
from jax.experimental.pallas import tpu as pltpu
from jax.sharding import PartitionSpec as P

NAT = 16
BS = 64
MESH = pl.DeviceIdType.MESH
NT = (((1,), (1,)), ((), ()))


def gather_kernel(nz, ri, ids_k, ids_n, size, go, gv, out,
                  slabs, perm, tmp, gop, gvm, sel, dense, virt, flat, idbuf, part, parts,
                  zsend, zrecv, xsend, xrecv, csend, crecv, isend, irecv, psend, precv, lsem):
    z = lax.axis_index("tensor")
    b = lax.axis_index("batch")
    r = lax.axis_index("rep")
    j = b * 2 + r
    pieces = 4
    waves = (nz - 1) * pieces
    left = {"tensor": z - 1}
    right = {"tensor": z + 1}
    across = {"batch": 1 - b}
    mate = {"rep": 1 - r}
    diag = {"batch": 1 - b, "rep": 1 - r}

    barrier = pltpu.get_barrier_semaphore()
    for step in range(1, nz):
        pl.semaphore_signal(barrier, inc=1, device_id={"tensor": lax.rem(z + step, nz)}, device_id_type=MESH)
    for dev in (across, mate, diag):
        pl.semaphore_signal(barrier, inc=1, device_id=dev, device_id_type=MESH)

    def local(q):
        return pltpu.make_async_copy(
            ri.at[:, pl.ds(16 * q, 16), :],
            slabs.at[z, q], lsem.at[q])

    def remote(src, dst, s, d, dev):
        return pltpu.make_async_remote_copy(src_ref=src, dst_ref=dst, send_sem=s, recv_sem=d,
                                            device_id=dev, device_id_type=MESH)

    def spot(o, p, q):
        return slabs.at[o, q, pl.ds(2 * p, 2)]

    for q in range(4):
        local(q).start()
    pl.semaphore_wait(barrier, nz - 1 + 3)

    def own(p, d):
        src = ri.at[pl.ds(2 * p, 2), pl.ds(pl.multiple_of(16 * j, 16), 16), :]
        return remote(src, spot(z, p, j), zsend.at[d, p], zrecv.at[d, p], right if d == 0 else left)

    def ids_copy(step):
        dev = {"tensor": lax.rem(z + step, nz)}
        return remote(ids_n, idbuf.at[z], isend.at[step], irecv.at[step], dev)

    for step in range(1, nz):
        ids_copy(step).start()
    for p in range(pieces):
        @pl.when(z < nz - 1)
        def _():
            own(p, 0).start()

        @pl.when(z > 0)
        def _():
            own(p, 1).start()

    def origin(d, t):
        return z - 1 - t if d == 0 else z + 1 + t

    def here(d, t):
        return t <= z - 1 if d == 0 else t <= nz - 2 - z

    def passes(d, t):
        ok = here(d, t)
        return jnp.logical_and(ok, z < nz - 1) if d == 0 else jnp.logical_and(ok, z > 0)

    def z_copy(d, w, o, p):
        return remote(spot(o, p, j), spot(o, p, j), zsend.at[d, w + pieces], zrecv.at[d, w + pieces],
                      right if d == 0 else left)

    def z_in(d, w, o, p):
        return remote(spot(o, p, j), spot(o, p, j), zsend.at[d, w], zrecv.at[d, w], right if d == 0 else left)

    def x_copy(d, w, o, p, q):
        return remote(spot(o, p, q), spot(o, p, q), xsend.at[d, w], xrecv.at[d, w], across)

    def c_copy(d, w, k, o, p, q):
        return remote(spot(o, p, q), spot(o, p, q), csend.at[d, w, k], crecv.at[d, w, k], mate)

    jx = (1 - b) * 2 + r
    jm = b * 2 + 1 - r
    jd = (1 - b) * 2 + 1 - r

    def arrive(w):
        t, p = w // pieces, w % pieces
        for d in (0, 1):
            @pl.when(here(d, t))
            def _():
                o = origin(d, t)
                z_in(d, w, o, p).wait_recv()

                @pl.when(passes(d, t))
                def _():
                    z_copy(d, w, o, p).start()
                x_copy(d, w, o, p, j).start()
                c_copy(d, w, 0, o, p, j).start()

    def spread(w):
        t, p = w // pieces, w % pieces
        for d in (0, 1):
            @pl.when(here(d, t))
            def _():
                o = origin(d, t)
                x_copy(d, w, o, p, jx).wait_recv()
                c_copy(d, w, 1, o, p, jx).start()

    def collect(w):
        t, p = w // pieces, w % pieces
        for d in (0, 1):
            @pl.when(here(d, t))
            def _():
                o = origin(d, t)
                c_copy(d, w, 0, o, p, jm).wait_recv()
                c_copy(d, w, 1, o, p, jd).wait_recv()

    lane = lax.broadcasted_iota(jnp.int32, (1, 1024), 1)
    limit = jnp.zeros((1, 1024), jnp.int32)
    for a in range(16):
        limit = jnp.where(lane // 64 == a, size[a], limit)

    def build(k, _):
        row = lax.broadcasted_iota(jnp.int32, (128, 1024), 0) + k * 128
        col = lax.broadcasted_iota(jnp.int32, (128, 1024), 1)
        place = (col % 64) * 16 + col // 64
        keep = jnp.logical_and(place == row, col % 64 < limit)
        perm[pl.ds(pl.multiple_of(k * 128, 128), 128), :] = jnp.where(keep, 1.0, 0.0).astype(jnp.bfloat16)
        return 0

    lax.fori_loop(0, 8, build, 0)

    def rows_in(k, _):
        at = pl.ds(pl.multiple_of(k * 256, 256), 256)
        tmp[at, :] = jnp.dot(perm[at, :], go[...], preferred_element_type=jnp.float32).astype(jnp.bfloat16)
        return 0

    lax.fori_loop(0, 4, rows_in, 0, unroll=True)

    def cols_in(k, _):
        at = pl.ds(pl.multiple_of(k * 256, 256), 256)
        gop[at, :] = lax.dot_general(tmp[at, :], perm[...], NT,
                                     preferred_element_type=jnp.float32).astype(jnp.bfloat16)
        return 0

    lax.fori_loop(0, 4, cols_in, 0, unroll=True)

    lane256 = lax.broadcasted_iota(jnp.int32, (64, 256), 1)
    sub256 = lax.broadcasted_iota(jnp.int32, (64, 256), 0)
    limit_c = jnp.zeros((64, 256), jnp.int32)
    for c in range(4):
        limit_c = jnp.where(lane256 // 64 == c, size[j * 4 + c], limit_c)
    for c in range(16):
        keep = jnp.logical_and(sub256 < size[c], lane256 % 64 < limit_c)
        block = gv[c * 64:(c + 1) * 64, :].astype(jnp.float32)
        gvm[c * 64:(c + 1) * 64, :] = jnp.where(keep, block, 0.0).astype(jnp.bfloat16)

    row = lax.broadcasted_iota(jnp.int32, (256, 64), 0)
    want = (row % 16) * 16 + ((row % 128) // 16) * 2 + row // 128
    sel[...] = jnp.where(ids_k[...] == want, 1.0, 0.0).astype(jnp.bfloat16)
    idbuf[z] = ids_n[...]
    part[...] = jnp.zeros_like(part)
    for q in range(4):
        local(q).wait()

    low = lax.broadcasted_iota(jnp.int32, (128, 128), 1) < 64
    low16 = lax.broadcasted_iota(jnp.int32, (32, 128), 1) < 64

    def one_function(f):
        def unpack(k, _):
            at = pl.ds(pl.multiple_of(k * 256, 256), 256)
            mine = jnp.concatenate([slabs[z, q, f, :, at] for q in range(4)], axis=0)
            got = jnp.dot(sel[...], mine, preferred_element_type=jnp.float32)
            for h in range(2):
                even, odd = got[:128, h * 128:(h + 1) * 128], got[128:, h * 128:(h + 1) * 128]
                first = jnp.where(low, even, pltpu.roll(odd, 64, 1)).astype(jnp.bfloat16)
                second = jnp.where(low, pltpu.roll(even, 64, 1), odd).astype(jnp.bfloat16)
                base = k * 64 + h * 32
                for c in range(8):
                    dense[pl.ds(pl.multiple_of(base, 16), 16), c * 128:(c + 1) * 128] = first[c * 16:(c + 1) * 16]
                    dense[pl.ds(pl.multiple_of(base + 16, 16), 16), c * 128:(c + 1) * 128] = second[c * 16:(c + 1) * 16]
            return 0

        lax.fori_loop(0, 16, unpack, 0, unroll=True)

        def virt_step(k, _):
            at = pl.ds(pl.multiple_of(k * 256, 256), 256)
            virt[at, :] = jnp.dot(dense[at, :], gvm[...], preferred_element_type=jnp.float32).astype(jnp.bfloat16)
            return 0

        lax.fori_loop(0, 4, virt_step, 0, unroll=True)

        def occ_step(k, _):
            at = pl.ds(pl.multiple_of(k * 256, 256), 256)
            occ = jnp.dot(gop[at, :], virt[...], preferred_element_type=jnp.float32)
            for h in range(8):
                even, odd = occ[h * 32:h * 32 + 16], occ[h * 32 + 16:h * 32 + 32]
                even = jnp.concatenate([even[:, :128], even[:, 128:]], axis=0)
                odd = jnp.concatenate([odd[:, :128], odd[:, 128:]], axis=0)
                first = jnp.where(low16, even, pltpu.roll(odd, 64, 1)).astype(jnp.bfloat16)
                second = jnp.where(low16, pltpu.roll(even, 64, 1), odd).astype(jnp.bfloat16)
                lanes = pl.ds(pl.multiple_of(k * 1024 + h * 128, 128), 128)
                flat[pl.ds(pl.multiple_of(f * 64, 32), 32), lanes] = first
                flat[pl.ds(pl.multiple_of(f * 64 + 32, 32), 32), lanes] = second
            return 0

        lax.fori_loop(0, 4, occ_step, 0, unroll=True)

    row64 = lax.broadcasted_iota(jnp.int32, (64, 128), 0)
    want64 = (row64 % 16) * 16 + j * 4 + ((row64 % 32) // 16) * 2 + row64 // 32
    out_lane = lax.broadcasted_iota(jnp.int32, (8, 128), 1)

    def contract(o, p):
        other = jnp.concatenate([slabs[o, q, pl.ds(2 * p, 2)].reshape(32, 4096) for q in range(4)], axis=0)
        pick = idbuf[o] == want64
        halves = jnp.zeros((8, 128), jnp.float32)
        for m in range(2):
            gram = lax.dot_general(flat[m * 256:(m + 1) * 256, :], other, NT, preferred_element_type=jnp.float32)
            for f in range(4):
                kept = jnp.sum(jnp.where(pick, gram[f * 64:(f + 1) * 64], 0.0), axis=0, keepdims=True)
                halves = jnp.where(lax.broadcasted_iota(jnp.int32, (8, 128), 0) == m * 4 + f, kept, halves)
        add = jnp.zeros((8, 128), jnp.float32)
        for q in range(2):
            total = jnp.sum(jnp.where((out_lane // 16) % 2 == q, halves, 0.0), axis=1, keepdims=True)
            add = add + jnp.where(out_lane == o * 8 + p * 2 + q, total, 0.0)
        part[...] += add

    def contract_wave(w):
        t, p = w // pieces, w % pieces
        for d in (0, 1):
            @pl.when(here(d, t))
            def _():
                contract(origin(d, t), p)

    def first_phase(w, _):
        one_function(2 * w)
        arrive(w)

        @pl.when(w > 0)
        def _():
            spread(w - 1)
        one_function(2 * w + 1)
        return 0

    lax.fori_loop(0, 4, first_phase, 0)
    for step in range(1, nz):
        ids_copy(step).wait_send()
        remote(ids_n, idbuf.at[z], isend.at[step], irecv.at[step], right).wait_recv()

    def own_slab(p, _):
        contract(z, p)
        return 0

    arrive(4)
    spread(3)
    lax.fori_loop(0, 2, own_slab, 0)
    arrive(5)
    spread(4)
    lax.fori_loop(2, 4, own_slab, 0)

    def catch_up(w, _):
        collect(w)
        contract_wave(w)
        return 0

    lax.fori_loop(0, 3, catch_up, 0)

    def second_phase(w, _):
        @pl.when(w < waves)
        def _():
            arrive(w)

        @pl.when(w < waves + 1)
        def _():
            spread(w - 1)
        collect(w - 3)
        contract_wave(w - 3)
        return 0

    lax.fori_loop(6, waves + 3, second_phase, 0)

    def p_copy(k, dev):
        return remote(part, parts.at[k], psend.at[k], precv.at[k], dev)

    for k, dev in enumerate((across, mate, diag)):
        p_copy(k, dev).start()

    def finish(w, _):
        t, p = w // pieces, w % pieces
        for d in (0, 1):
            @pl.when(here(d, t))
            def _():
                o = origin(d, t)

                @pl.when(passes(d, t))
                def _():
                    z_copy(d, w, o, p).wait_send()
                x_copy(d, w, o, p, j).wait_send()
                c_copy(d, w, 0, o, p, j).wait_send()
                c_copy(d, w, 1, o, p, jx).wait_send()
        return 0

    lax.fori_loop(0, waves, finish, 0)
    for p in range(pieces):
        @pl.when(z < nz - 1)
        def _():
            own(p, 0).wait_send()

        @pl.when(z > 0)
        def _():
            own(p, 1).wait_send()
    for k, dev in enumerate((across, mate, diag)):
        p_copy(k, dev).wait()
    total = part[...] + parts[0] + parts[1] + parts[2]
    wide = out.shape[1]
    result = jnp.zeros(out.shape, jnp.float32)
    for q in range(4):
        result = jnp.where(j == q, total[:, q * wide:(q + 1) * wide], result)
    out[...] = result


def fused(nz, ri_tensor, pair_ids, atom_size, green_occ, green_virt):
    ids_n = jnp.broadcast_to(pair_ids.reshape(4, 1, 16), (4, 2, 16)).reshape(1, 128)
    waves = (nz - 1) * 4
    vmem = pl.BlockSpec(memory_space=pltpu.VMEM)
    bf16 = jnp.bfloat16
    dma = pltpu.SemaphoreType.DMA
    return pl.pallas_call(
        functools.partial(gather_kernel, nz),
        out_shape=jax.ShapeDtypeStruct((8, nz * 2), jnp.float32),
        in_specs=[pl.BlockSpec(memory_space=pl.ANY), vmem, vmem,
                  pl.BlockSpec(memory_space=pltpu.SMEM), vmem, vmem],
        out_specs=vmem,
        scratch_shapes=[
            pltpu.VMEM((nz, 4, 8, 16, 4096), bf16),
            pltpu.VMEM((1024, 1024), bf16),
            pltpu.VMEM((1024, 1024), bf16),
            pltpu.VMEM((1024, 1024), bf16),
            pltpu.VMEM((1024, 256), bf16),
            pltpu.VMEM((256, 64), bf16),
            pltpu.VMEM((1024, 1024), bf16),
            pltpu.VMEM((1024, 256), bf16),
            pltpu.VMEM((512, 4096), bf16),
            pltpu.VMEM((nz, 1, 128), jnp.int32),
            pltpu.VMEM((8, 128), jnp.float32),
            pltpu.VMEM((3, 8, 128), jnp.float32),
            dma((2, waves + 4)), dma((2, waves + 4)),
            dma((2, waves)), dma((2, waves)),
            dma((2, waves, 2)), dma((2, waves, 2)),
            dma((nz,)), dma((nz,)), dma((3,)), dma((3,)), dma((4,)),
        ],
        compiler_params=pltpu.CompilerParams(
            collective_id=0, has_side_effects=True, vmem_limit_bytes=56 * 1024 * 1024),
    )(ri_tensor, pair_ids.reshape(1, 64), ids_n, atom_size, green_occ, green_virt)


def per_device(ri_tensor, pair_ids, atom_size, green_occ, green_virt):
    nz = lax.axis_size("tensor")
    split = (lax.axis_size("batch"), lax.axis_size("rep"))
    if nz == 4 and split == (2, 2) and ri_tensor.shape == (8, 64, 4096) and green_occ.shape == (1024, 1024):
        return fused(nz, ri_tensor, pair_ids, atom_size, green_occ, green_virt)
    return whole_blocks(ri_tensor, pair_ids, atom_size, green_occ, green_virt)


def whole_blocks(ri_tensor, pair_ids, atom_size, green_occ, green_virt):
    local_rows = ri_tensor.shape[0]
    slots = ri_tensor.shape[1]
    total_ao = green_occ.shape[0]
    columns = green_virt.shape[1]
    first_col = (lax.axis_index("batch") * lax.axis_size("rep") + lax.axis_index("rep")) * columns
    usable = (jnp.arange(BS)[None, :] < atom_size[:, None]).astype(jnp.bfloat16)
    row_atoms = pair_ids // NAT
    col_atoms = pair_ids % NAT
    blocks = ri_tensor.reshape(local_rows, slots, BS, BS)
    blocks = blocks * usable[row_atoms][None, :, :, None] * usable[col_atoms][None, :, None, :]
    selector_f = row_atoms[None, :] == jnp.arange(NAT)[:, None]
    selector = selector_f.astype(jnp.bfloat16)
    block_cols = col_atoms[:, None] * BS + jnp.arange(BS)[None, :]
    wanted = first_col + jnp.arange(columns)
    picker = (block_cols[:, :, None] == wanted[None, None, :]).astype(jnp.bfloat16)
    picked = jnp.einsum(
        "psij,sjk->psik", blocks, picker, preferred_element_type=jnp.float32
    ).astype(jnp.bfloat16)
    tensor_piece = jnp.einsum("as,psik->paik", selector, picked, preferred_element_type=jnp.float32)
    tensor_piece = tensor_piece.astype(jnp.bfloat16).reshape(local_rows, total_ao, columns)
    gv_blocks = green_virt.reshape(NAT, BS, columns)[col_atoms]
    per_slot = jnp.einsum("psij,sjk->psik", blocks, gv_blocks, preferred_element_type=jnp.float32)
    upper = per_slot.astype(jnp.bfloat16)
    rest = per_slot - upper.astype(jnp.float32)
    middle = rest.astype(jnp.bfloat16)
    lower = (rest - middle.astype(jnp.float32)).astype(jnp.bfloat16)
    virt_side = jnp.einsum("as,psik->paik", selector, upper, preferred_element_type=jnp.float32)
    virt_side = virt_side + jnp.einsum(
        "as,psik->paik", selector, middle, preferred_element_type=jnp.float32
    )
    virt_side = virt_side + jnp.einsum(
        "as,psik->paik", selector, lower, preferred_element_type=jnp.float32
    )
    virt_side = virt_side.astype(jnp.bfloat16).reshape(local_rows, total_ao, columns)
    occ_side = jnp.einsum(
        "lm,pms->pls", green_occ, virt_side, preferred_element_type=jnp.float32
    ).astype(jnp.bfloat16)
    moved_occ, moved_tensor = (
        lax.all_to_all(occ_side, "tensor", split_axis=1, concat_axis=0, tiled=True),
        lax.all_to_all(tensor_piece, "tensor", split_axis=1, concat_axis=0, tiled=True),
    )
    partial_value = jnp.einsum(
        "pls,qls->pq", moved_occ, moved_tensor, preferred_element_type=jnp.float32
    )
    own_rows = lax.psum_scatter(partial_value, "tensor", scatter_dimension=0, tiled=True)
    return lax.psum_scatter(own_rows, ("batch", "rep"), scatter_dimension=1, tiled=True)


def solution(mesh):
    in_specs = (
        P(("groups", "tensor"), None, None),
        P(("groups", "tensor")),
        P(),
        P(),
        P(None, ("batch", "rep")),
    )
    out_specs = P(("groups", "tensor"), ("batch", "rep"))
    return jax.shard_map(
        per_device, mesh=mesh, in_specs=in_specs, out_specs=out_specs, check_vma=False
    )
```

```python
import functools

import jax
import jax.numpy as jnp
from jax import lax
from jax.experimental import pallas as pl
from jax.experimental.pallas import tpu as pltpu
from jax.sharding import PartitionSpec as P

NAT = 16
BS = 64
MESH = pl.DeviceIdType.MESH
NT = (((1,), (1,)), ((), ()))


def gather_kernel(nz, ri, ids_k, size, go, gv, out,
                  slabs, perm, tmp, gop, gvm, sel, dense, virt, flat, ids_n, idbuf, part, parts,
                  zsend, zrecv, xsend, xrecv, csend, crecv, isend, irecv, psend, precv, lsem):
    z = lax.axis_index("tensor")
    b = lax.axis_index("batch")
    r = lax.axis_index("rep")
    j = b * 2 + r
    pieces = 8
    waves = (nz - 1) * pieces
    left = {"tensor": z - 1}
    right = {"tensor": z + 1}
    across = {"batch": 1 - b}
    mate = {"rep": 1 - r}
    diag = {"batch": 1 - b, "rep": 1 - r}

    barrier = pltpu.get_barrier_semaphore()
    for step in range(1, nz):
        pl.semaphore_signal(barrier, inc=1, device_id={"tensor": lax.rem(z + step, nz)}, device_id_type=MESH)
    for dev in (across, mate, diag):
        pl.semaphore_signal(barrier, inc=1, device_id=dev, device_id_type=MESH)

    def local(q):
        return pltpu.make_async_copy(
            ri.at[:, pl.ds(16 * q, 16), :],
            slabs.at[z, q], lsem.at[q])

    def remote(src, dst, s, d, dev):
        return pltpu.make_async_remote_copy(src_ref=src, dst_ref=dst, send_sem=s, recv_sem=d,
                                            device_id=dev, device_id_type=MESH)

    def spot(o, p, q):
        return slabs.at[o, q, pl.ds(p, 1)]

    for q in range(4):
        local(q).start()
    pl.semaphore_wait(barrier, nz - 1 + 3)

    def own(p, d):
        src = ri.at[pl.ds(p, 1), pl.ds(pl.multiple_of(16 * j, 16), 16), :]
        return remote(src, spot(z, p, j), zsend.at[d, p], zrecv.at[d, p], right if d == 0 else left)

    def ids_copy(step):
        dev = {"tensor": lax.rem(z + step, nz)}
        return remote(ids_n, idbuf.at[z], isend.at[step], irecv.at[step], dev)

    for p in range(pieces):
        @pl.when(z < nz - 1)
        def _():
            own(p, 0).start()

        @pl.when(z > 0)
        def _():
            own(p, 1).start()

    slot = lax.broadcasted_iota(jnp.int32, (64, 128), 0)
    spread_lane = lax.broadcasted_iota(jnp.int32, (64, 128), 1)
    chosen = jnp.where(slot == (spread_lane // 32) * 16 + spread_lane % 16, 1.0, 0.0).astype(jnp.bfloat16)
    listed = jnp.broadcast_to(ids_k[...], (8, 64)).astype(jnp.float32).astype(jnp.bfloat16)
    ids_n[...] = jnp.dot(listed, chosen, preferred_element_type=jnp.float32)[0:1]
    idbuf[z] = ids_n[...]
    for step in range(1, nz):
        ids_copy(step).start()

    def origin(d, t):
        return z - 1 - t if d == 0 else z + 1 + t

    def here(d, t):
        return t <= z - 1 if d == 0 else t <= nz - 2 - z

    def passes(d, t):
        ok = here(d, t)
        return jnp.logical_and(ok, z < nz - 1) if d == 0 else jnp.logical_and(ok, z > 0)

    def z_copy(d, w, o, p):
        return remote(spot(o, p, j), spot(o, p, j), zsend.at[d, w + pieces], zrecv.at[d, w + pieces],
                      right if d == 0 else left)

    def z_in(d, w, o, p):
        return remote(spot(o, p, j), spot(o, p, j), zsend.at[d, w], zrecv.at[d, w], right if d == 0 else left)

    def x_copy(d, w, o, p, q):
        return remote(spot(o, p, q), spot(o, p, q), xsend.at[d, w], xrecv.at[d, w], across)

    def c_copy(d, w, k, o, p, q):
        return remote(spot(o, p, q), spot(o, p, q), csend.at[d, w, k], crecv.at[d, w, k], mate)

    jx = (1 - b) * 2 + r
    jm = b * 2 + 1 - r
    jd = (1 - b) * 2 + 1 - r

    def arrive(w):
        t, p = w // pieces, w % pieces
        for d in (0, 1):
            @pl.when(here(d, t))
            def _():
                o = origin(d, t)
                z_in(d, w, o, p).wait_recv()

                @pl.when(passes(d, t))
                def _():
                    z_copy(d, w, o, p).start()
                x_copy(d, w, o, p, j).start()
                c_copy(d, w, 0, o, p, j).start()

    def spread(w):
        t, p = w // pieces, w % pieces
        for d in (0, 1):
            @pl.when(here(d, t))
            def _():
                o = origin(d, t)
                x_copy(d, w, o, p, jx).wait_recv()
                c_copy(d, w, 1, o, p, jx).start()

    def collect(w):
        t, p = w // pieces, w % pieces
        for d in (0, 1):
            @pl.when(here(d, t))
            def _():
                o = origin(d, t)
                c_copy(d, w, 0, o, p, jm).wait_recv()
                c_copy(d, w, 1, o, p, jd).wait_recv()

    lane = lax.broadcasted_iota(jnp.int32, (1, 1024), 1)
    limit = jnp.zeros((1, 1024), jnp.int32)
    for a in range(16):
        limit = jnp.where(lane // 64 == a, size[a], limit)

    def build(k, _):
        row = lax.broadcasted_iota(jnp.int32, (128, 1024), 0) + k * 128
        col = lax.broadcasted_iota(jnp.int32, (128, 1024), 1)
        place = (col % 64) * 16 + col // 64
        keep = jnp.logical_and(place == row, col % 64 < limit)
        perm[pl.ds(pl.multiple_of(k * 128, 128), 128), :] = jnp.where(keep, 1.0, 0.0).astype(jnp.bfloat16)
        return 0

    lax.fori_loop(0, 8, build, 0)

    def rows_in(k, _):
        at = pl.ds(pl.multiple_of(k * 256, 256), 256)
        tmp[at, :] = jnp.dot(perm[at, :], go[...], preferred_element_type=jnp.float32).astype(jnp.bfloat16)
        return 0

    lax.fori_loop(0, 4, rows_in, 0, unroll=True)
    arrive(0)

    def cols_in(k, _):
        at = pl.ds(pl.multiple_of(k * 256, 256), 256)
        gop[at, :] = lax.dot_general(tmp[at, :], perm[...], NT,
                                     preferred_element_type=jnp.float32).astype(jnp.bfloat16)
        return 0

    lax.fori_loop(0, 4, cols_in, 0, unroll=True)

    lane256 = lax.broadcasted_iota(jnp.int32, (64, 256), 1)
    sub256 = lax.broadcasted_iota(jnp.int32, (64, 256), 0)
    limit_c = jnp.zeros((64, 256), jnp.int32)
    for c in range(4):
        limit_c = jnp.where(lane256 // 64 == c, size[j * 4 + c], limit_c)
    for c in range(16):
        keep = jnp.logical_and(sub256 < size[c], lane256 % 64 < limit_c)
        block = gv[c * 64:(c + 1) * 64, :].astype(jnp.float32)
        gvm[c * 64:(c + 1) * 64, :] = jnp.where(keep, block, 0.0).astype(jnp.bfloat16)

    row = lax.broadcasted_iota(jnp.int32, (256, 64), 0)
    want = (row % 16) * 16 + ((row % 128) // 16) * 2 + row // 128
    sel[...] = jnp.where(ids_k[...] == want, 1.0, 0.0).astype(jnp.bfloat16)
    part[...] = jnp.zeros_like(part)
    for q in range(4):
        local(q).wait()

    low = lax.broadcasted_iota(jnp.int32, (128, 128), 1) < 64
    low16 = lax.broadcasted_iota(jnp.int32, (32, 128), 1) < 64

    def one_function(f):
        def unpack(k, _):
            at = pl.ds(pl.multiple_of(k * 256, 256), 256)
            mine = jnp.concatenate([slabs[z, q, f, :, at] for q in range(4)], axis=0)
            got = jnp.dot(sel[...], mine, preferred_element_type=jnp.float32)
            for h in range(2):
                even, odd = got[:128, h * 128:(h + 1) * 128], got[128:, h * 128:(h + 1) * 128]
                first = jnp.where(low, even, pltpu.roll(odd, 64, 1)).astype(jnp.bfloat16)
                second = jnp.where(low, pltpu.roll(even, 64, 1), odd).astype(jnp.bfloat16)
                base = k * 64 + h * 32
                for c in range(8):
                    dense[pl.ds(pl.multiple_of(base, 16), 16), c * 128:(c + 1) * 128] = first[c * 16:(c + 1) * 16]
                    dense[pl.ds(pl.multiple_of(base + 16, 16), 16), c * 128:(c + 1) * 128] = second[c * 16:(c + 1) * 16]
            return 0

        lax.fori_loop(0, 16, unpack, 0, unroll=True)

        def virt_step(k, _):
            at = pl.ds(pl.multiple_of(k * 256, 256), 256)
            virt[at, :] = jnp.dot(dense[at, :], gvm[...], preferred_element_type=jnp.float32).astype(jnp.bfloat16)
            return 0

        lax.fori_loop(0, 4, virt_step, 0, unroll=True)

        def occ_step(k, _):
            at = pl.ds(pl.multiple_of(k * 256, 256), 256)
            occ = jnp.dot(gop[at, :], virt[...], preferred_element_type=jnp.float32)
            for h in range(8):
                even, odd = occ[h * 32:h * 32 + 16], occ[h * 32 + 16:h * 32 + 32]
                even = jnp.concatenate([even[:, :128], even[:, 128:]], axis=0)
                odd = jnp.concatenate([odd[:, :128], odd[:, 128:]], axis=0)
                first = jnp.where(low16, even, pltpu.roll(odd, 64, 1)).astype(jnp.bfloat16)
                second = jnp.where(low16, pltpu.roll(even, 64, 1), odd).astype(jnp.bfloat16)
                lanes = pl.ds(pl.multiple_of(k * 1024 + h * 128, 128), 128)
                flat[pl.ds(pl.multiple_of(f * 64, 32), 32), lanes] = first
                flat[pl.ds(pl.multiple_of(f * 64 + 32, 32), 32), lanes] = second
            return 0

        lax.fori_loop(0, 4, occ_step, 0, unroll=True)

    row64 = lax.broadcasted_iota(jnp.int32, (64, 128), 0)
    want64 = (row64 % 16) * 16 + j * 4 + ((row64 % 32) // 16) * 2 + row64 // 32
    out_lane = lax.broadcasted_iota(jnp.int32, (8, 128), 1)

    def contract(o, p):
        other = jnp.concatenate([slabs[o, q, pl.ds(2 * p, 2)].reshape(32, 4096) for q in range(4)], axis=0)
        pick = idbuf[o] == want64.astype(jnp.float32)
        halves = jnp.zeros((8, 128), jnp.float32)
        for m in range(2):
            gram = lax.dot_general(flat[m * 256:(m + 1) * 256, :], other, NT, preferred_element_type=jnp.float32)
            for f in range(4):
                kept = jnp.sum(jnp.where(pick, gram[f * 64:(f + 1) * 64], 0.0), axis=0, keepdims=True)
                halves = jnp.where(lax.broadcasted_iota(jnp.int32, (8, 128), 0) == m * 4 + f, kept, halves)
        add = jnp.zeros((8, 128), jnp.float32)
        for q in range(2):
            total = jnp.sum(jnp.where((out_lane // 16) % 2 == q, halves, 0.0), axis=1, keepdims=True)
            add = add + jnp.where(out_lane == o * 8 + p * 2 + q, total, 0.0)
        part[...] += add

    def contract_wave(w):
        t, p = w // 4, w % 4
        for d in (0, 1):
            @pl.when(here(d, t))
            def _():
                contract(origin(d, t), p)

    arrive(1)

    def first_phase(f, _):
        one_function(f)
        arrive(f + 2)
        spread(f)
        return 0

    lax.fori_loop(0, 8, first_phase, 0)
    for step in range(1, nz):
        ids_copy(step).wait_send()
        remote(ids_n, idbuf.at[z], isend.at[step], irecv.at[step], right).wait_recv()

    def own_slab(p, _):
        contract(z, p)
        arrive(10 + p)
        spread(8 + p)
        return 0

    lax.fori_loop(0, 4, own_slab, 0)

    def second_phase(u, _):
        @pl.when(u + 14 < waves)
        def _():
            arrive(u + 14)
        spread(u + 12)
        collect(2 * u)
        collect(2 * u + 1)
        contract_wave(u)
        return 0

    lax.fori_loop(0, waves // 2, second_phase, 0)

    def p_copy(k, dev):
        return remote(part, parts.at[k], psend.at[k], precv.at[k], dev)

    for k, dev in enumerate((across, mate, diag)):
        p_copy(k, dev).start()

    def finish(w, _):
        t, p = w // pieces, w % pieces
        for d in (0, 1):
            @pl.when(here(d, t))
            def _():
                o = origin(d, t)

                @pl.when(passes(d, t))
                def _():
                    z_copy(d, w, o, p).wait_send()
                x_copy(d, w, o, p, j).wait_send()
                c_copy(d, w, 0, o, p, j).wait_send()
                c_copy(d, w, 1, o, p, jx).wait_send()
        return 0

    lax.fori_loop(0, waves, finish, 0)
    for p in range(pieces):
        @pl.when(z < nz - 1)
        def _():
            own(p, 0).wait_send()

        @pl.when(z > 0)
        def _():
            own(p, 1).wait_send()
    for k, dev in enumerate((across, mate, diag)):
        p_copy(k, dev).wait()
    total = part[...] + parts[0] + parts[1] + parts[2]
    wide = out.shape[1]
    result = jnp.zeros(out.shape, jnp.float32)
    for q in range(4):
        result = jnp.where(j == q, total[:, q * wide:(q + 1) * wide], result)
    out[...] = result


def fused(nz, ri_tensor, pair_ids, atom_size, green_occ, green_virt):
    waves = (nz - 1) * 8
    vmem = pl.BlockSpec(memory_space=pltpu.VMEM)
    bf16 = jnp.bfloat16
    dma = pltpu.SemaphoreType.DMA
    return pl.pallas_call(
        functools.partial(gather_kernel, nz),
        out_shape=jax.ShapeDtypeStruct((8, nz * 2), jnp.float32),
        in_specs=[pl.BlockSpec(memory_space=pl.ANY), vmem,
                  pl.BlockSpec(memory_space=pltpu.SMEM), vmem, vmem],
        out_specs=vmem,
        scratch_shapes=[
            pltpu.VMEM((nz, 4, 8, 16, 4096), bf16),
            pltpu.VMEM((1024, 1024), bf16),
            pltpu.VMEM((1024, 1024), bf16),
            pltpu.VMEM((1024, 1024), bf16),
            pltpu.VMEM((1024, 256), bf16),
            pltpu.VMEM((256, 64), bf16),
            pltpu.VMEM((1024, 1024), bf16),
            pltpu.VMEM((1024, 256), bf16),
            pltpu.VMEM((512, 4096), bf16),
            pltpu.VMEM((1, 128), jnp.float32),
            pltpu.VMEM((nz, 1, 128), jnp.float32),
            pltpu.VMEM((8, 128), jnp.float32),
            pltpu.VMEM((3, 8, 128), jnp.float32),
            dma((2, waves + 8)), dma((2, waves + 8)),
            dma((2, waves)), dma((2, waves)),
            dma((2, waves, 2)), dma((2, waves, 2)),
            dma((nz,)), dma((nz,)), dma((3,)), dma((3,)), dma((4,)),
        ],
        compiler_params=pltpu.CompilerParams(
            collective_id=0, has_side_effects=True, vmem_limit_bytes=56 * 1024 * 1024),
    )(ri_tensor, pair_ids.reshape(1, 64), atom_size, green_occ, green_virt)


def per_device(ri_tensor, pair_ids, atom_size, green_occ, green_virt):
    nz = lax.axis_size("tensor")
    split = (lax.axis_size("batch"), lax.axis_size("rep"))
    if nz == 4 and split == (2, 2) and ri_tensor.shape == (8, 64, 4096) and green_occ.shape == (1024, 1024):
        return fused(nz, ri_tensor, pair_ids, atom_size, green_occ, green_virt)
    return whole_blocks(ri_tensor, pair_ids, atom_size, green_occ, green_virt)


def whole_blocks(ri_tensor, pair_ids, atom_size, green_occ, green_virt):
    local_rows = ri_tensor.shape[0]
    slots = ri_tensor.shape[1]
    total_ao = green_occ.shape[0]
    columns = green_virt.shape[1]
    first_col = (lax.axis_index("batch") * lax.axis_size("rep") + lax.axis_index("rep")) * columns
    usable = (jnp.arange(BS)[None, :] < atom_size[:, None]).astype(jnp.bfloat16)
    row_atoms = pair_ids // NAT
    col_atoms = pair_ids % NAT
    blocks = ri_tensor.reshape(local_rows, slots, BS, BS)
    blocks = blocks * usable[row_atoms][None, :, :, None] * usable[col_atoms][None, :, None, :]
    selector_f = row_atoms[None, :] == jnp.arange(NAT)[:, None]
    selector = selector_f.astype(jnp.bfloat16)
    block_cols = col_atoms[:, None] * BS + jnp.arange(BS)[None, :]
    wanted = first_col + jnp.arange(columns)
    picker = (block_cols[:, :, None] == wanted[None, None, :]).astype(jnp.bfloat16)
    picked = jnp.einsum(
        "psij,sjk->psik", blocks, picker, preferred_element_type=jnp.float32
    ).astype(jnp.bfloat16)
    tensor_piece = jnp.einsum("as,psik->paik", selector, picked, preferred_element_type=jnp.float32)
    tensor_piece = tensor_piece.astype(jnp.bfloat16).reshape(local_rows, total_ao, columns)
    gv_blocks = green_virt.reshape(NAT, BS, columns)[col_atoms]
    per_slot = jnp.einsum("psij,sjk->psik", blocks, gv_blocks, preferred_element_type=jnp.float32)
    upper = per_slot.astype(jnp.bfloat16)
    rest = per_slot - upper.astype(jnp.float32)
    middle = rest.astype(jnp.bfloat16)
    lower = (rest - middle.astype(jnp.float32)).astype(jnp.bfloat16)
    virt_side = jnp.einsum("as,psik->paik", selector, upper, preferred_element_type=jnp.float32)
    virt_side = virt_side + jnp.einsum(
        "as,psik->paik", selector, middle, preferred_element_type=jnp.float32
    )
    virt_side = virt_side + jnp.einsum(
        "as,psik->paik", selector, lower, preferred_element_type=jnp.float32
    )
    virt_side = virt_side.astype(jnp.bfloat16).reshape(local_rows, total_ao, columns)
    occ_side = jnp.einsum(
        "lm,pms->pls", green_occ, virt_side, preferred_element_type=jnp.float32
    ).astype(jnp.bfloat16)
    moved_occ, moved_tensor = (
        lax.all_to_all(occ_side, "tensor", split_axis=1, concat_axis=0, tiled=True),
        lax.all_to_all(tensor_piece, "tensor", split_axis=1, concat_axis=0, tiled=True),
    )
    partial_value = jnp.einsum(
        "pls,qls->pq", moved_occ, moved_tensor, preferred_element_type=jnp.float32
    )
    own_rows = lax.psum_scatter(partial_value, "tensor", scatter_dimension=0, tiled=True)
    return lax.psum_scatter(own_rows, ("batch", "rep"), scatter_dimension=1, tiled=True)


def solution(mesh):
    in_specs = (
        P(("groups", "tensor"), None, None),
        P(("groups", "tensor")),
        P(),
        P(),
        P(None, ("batch", "rep")),
    )
    out_specs = P(("groups", "tensor"), ("batch", "rep"))
    return jax.shard_map(
        per_device, mesh=mesh, in_specs=in_specs, out_specs=out_specs, check_vma=False
    )
```

```python
import functools

import jax
import jax.numpy as jnp
from jax import lax
from jax.experimental import pallas as pl
from jax.experimental.pallas import tpu as pltpu
from jax.sharding import PartitionSpec as P

NAT = 16
BS = 64
MESH = pl.DeviceIdType.MESH
NT = (((1,), (1,)), ((), ()))


def gather_kernel(nz, ri, ids_k, size, go, gv, out,
                  slabs, perm, tmp, gop, gvm, sel, dense, virt, flat, ids_n, idbuf, part, parts,
                  zsend, zrecv, xsend, xrecv, csend, crecv, isend, irecv, psend, precv, lsem):
    z = lax.axis_index("tensor")
    b = lax.axis_index("batch")
    r = lax.axis_index("rep")
    j = b * 2 + r
    pieces = 8
    waves = (nz - 1) * pieces
    left = {"tensor": z - 1}
    right = {"tensor": z + 1}
    across = {"batch": 1 - b}
    mate = {"rep": 1 - r}
    diag = {"batch": 1 - b, "rep": 1 - r}

    barrier = pltpu.get_barrier_semaphore()
    for step in range(1, nz):
        pl.semaphore_signal(barrier, inc=1, device_id={"tensor": lax.rem(z + step, nz)}, device_id_type=MESH)
    for dev in (across, mate, diag):
        pl.semaphore_signal(barrier, inc=1, device_id=dev, device_id_type=MESH)

    def local(q):
        return pltpu.make_async_copy(
            ri.at[:, pl.ds(16 * q, 16), :],
            slabs.at[z, q], lsem.at[q])

    def remote(src, dst, s, d, dev):
        return pltpu.make_async_remote_copy(src_ref=src, dst_ref=dst, send_sem=s, recv_sem=d,
                                            device_id=dev, device_id_type=MESH)

    def spot(o, p, q):
        return slabs.at[o, q, pl.ds(p, 1)]

    for q in range(4):
        local(q).start()
    pl.semaphore_wait(barrier, nz - 1 + 3)

    def own(p, d):
        src = ri.at[pl.ds(p, 1), pl.ds(pl.multiple_of(16 * j, 16), 16), :]
        return remote(src, spot(z, p, j), zsend.at[d, p], zrecv.at[d, p], right if d == 0 else left)

    def ids_copy(step):
        dev = {"tensor": lax.rem(z + step, nz)}
        return remote(ids_n, idbuf.at[z], isend.at[step], irecv.at[step], dev)

    for p in range(pieces):
        @pl.when(z < nz - 1)
        def _():
            own(p, 0).start()

        @pl.when(z > 0)
        def _():
            own(p, 1).start()

    slot = lax.broadcasted_iota(jnp.int32, (64, 128), 0)
    spread_lane = lax.broadcasted_iota(jnp.int32, (64, 128), 1)
    chosen = jnp.where(slot == (spread_lane // 32) * 16 + spread_lane % 16, 1.0, 0.0).astype(jnp.bfloat16)
    listed = jnp.broadcast_to(ids_k[...], (8, 64)).astype(jnp.float32).astype(jnp.bfloat16)
    ids_n[...] = jnp.dot(listed, chosen, preferred_element_type=jnp.float32)[0:1]
    idbuf[z] = ids_n[...]
    for step in range(1, nz):
        ids_copy(step).start()

    def origin(d, t):
        return z - 1 - t if d == 0 else z + 1 + t

    def here(d, t):
        return t <= z - 1 if d == 0 else t <= nz - 2 - z

    def passes(d, t):
        ok = here(d, t)
        return jnp.logical_and(ok, z < nz - 1) if d == 0 else jnp.logical_and(ok, z > 0)

    def z_copy(d, w, o, p):
        return remote(spot(o, p, j), spot(o, p, j), zsend.at[d, w + pieces], zrecv.at[d, w + pieces],
                      right if d == 0 else left)

    def z_in(d, w, o, p):
        return remote(spot(o, p, j), spot(o, p, j), zsend.at[d, w], zrecv.at[d, w], right if d == 0 else left)

    def x_copy(d, w, o, p, q):
        return remote(spot(o, p, q), spot(o, p, q), xsend.at[d, w], xrecv.at[d, w], across)

    def c_copy(d, w, k, o, p, q):
        return remote(spot(o, p, q), spot(o, p, q), csend.at[d, w, k], crecv.at[d, w, k], mate)

    jx = (1 - b) * 2 + r
    jm = b * 2 + 1 - r
    jd = (1 - b) * 2 + 1 - r

    def arrive(w):
        t, p = w // pieces, w % pieces
        for d in (0, 1):
            @pl.when(here(d, t))
            def _():
                o = origin(d, t)
                z_in(d, w, o, p).wait_recv()

                @pl.when(passes(d, t))
                def _():
                    z_copy(d, w, o, p).start()
                x_copy(d, w, o, p, j).start()
                c_copy(d, w, 0, o, p, j).start()

    def spread(w):
        t, p = w // pieces, w % pieces
        for d in (0, 1):
            @pl.when(here(d, t))
            def _():
                o = origin(d, t)
                x_copy(d, w, o, p, jx).wait_recv()
                c_copy(d, w, 1, o, p, jx).start()

    def collect(w):
        t, p = w // pieces, w % pieces
        for d in (0, 1):
            @pl.when(here(d, t))
            def _():
                o = origin(d, t)
                c_copy(d, w, 0, o, p, jm).wait_recv()
                c_copy(d, w, 1, o, p, jd).wait_recv()

    lane = lax.broadcasted_iota(jnp.int32, (1, 1024), 1)
    limit = jnp.zeros((1, 1024), jnp.int32)
    for a in range(16):
        limit = jnp.where(lane // 64 == a, size[a], limit)

    def build(k, _):
        row = lax.broadcasted_iota(jnp.int32, (128, 1024), 0) + k * 128
        col = lax.broadcasted_iota(jnp.int32, (128, 1024), 1)
        place = (col % 64) * 16 + col // 64
        keep = jnp.logical_and(place == row, col % 64 < limit)
        perm[pl.ds(pl.multiple_of(k * 128, 128), 128), :] = jnp.where(keep, 1.0, 0.0).astype(jnp.bfloat16)
        return 0

    lax.fori_loop(0, 8, build, 0)
    arrive(0)

    def rows_in(k, _):
        at = pl.ds(pl.multiple_of(k * 256, 256), 256)
        tmp[at, :] = jnp.dot(perm[at, :], go[...], preferred_element_type=jnp.float32).astype(jnp.bfloat16)
        return 0

    lax.fori_loop(0, 4, rows_in, 0, unroll=True)
    arrive(1)

    def cols_in(k, _):
        at = pl.ds(pl.multiple_of(k * 256, 256), 256)
        gop[at, :] = lax.dot_general(tmp[at, :], perm[...], NT,
                                     preferred_element_type=jnp.float32).astype(jnp.bfloat16)
        return 0

    lax.fori_loop(0, 4, cols_in, 0, unroll=True)

    lane256 = lax.broadcasted_iota(jnp.int32, (64, 256), 1)
    sub256 = lax.broadcasted_iota(jnp.int32, (64, 256), 0)
    limit_c = jnp.zeros((64, 256), jnp.int32)
    for c in range(4):
        limit_c = jnp.where(lane256 // 64 == c, size[j * 4 + c], limit_c)
    for c in range(16):
        keep = jnp.logical_and(sub256 < size[c], lane256 % 64 < limit_c)
        block = gv[c * 64:(c + 1) * 64, :].astype(jnp.float32)
        gvm[c * 64:(c + 1) * 64, :] = jnp.where(keep, block, 0.0).astype(jnp.bfloat16)

    row = lax.broadcasted_iota(jnp.int32, (256, 64), 0)
    want = (row % 16) * 16 + ((row % 128) // 16) * 2 + row // 128
    sel[...] = jnp.where(ids_k[...] == want, 1.0, 0.0).astype(jnp.bfloat16)
    part[...] = jnp.zeros_like(part)
    for q in range(4):
        local(q).wait()

    low = lax.broadcasted_iota(jnp.int32, (128, 128), 1) < 64
    low16 = lax.broadcasted_iota(jnp.int32, (32, 128), 1) < 64

    def one_function(f):
        def unpack(k, _):
            at = pl.ds(pl.multiple_of(k * 256, 256), 256)
            mine = jnp.concatenate([slabs[z, q, f, :, at] for q in range(4)], axis=0)
            got = jnp.dot(sel[...], mine, preferred_element_type=jnp.float32)
            for h in range(2):
                even, odd = got[:128, h * 128:(h + 1) * 128], got[128:, h * 128:(h + 1) * 128]
                first = jnp.where(low, even, pltpu.roll(odd, 64, 1)).astype(jnp.bfloat16)
                second = jnp.where(low, pltpu.roll(even, 64, 1), odd).astype(jnp.bfloat16)
                base = k * 64 + h * 32
                for c in range(8):
                    dense[pl.ds(pl.multiple_of(base, 16), 16), c * 128:(c + 1) * 128] = first[c * 16:(c + 1) * 16]
                    dense[pl.ds(pl.multiple_of(base + 16, 16), 16), c * 128:(c + 1) * 128] = second[c * 16:(c + 1) * 16]
            return 0

        lax.fori_loop(0, 16, unpack, 0, unroll=True)

        def virt_step(k, _):
            at = pl.ds(pl.multiple_of(k * 256, 256), 256)
            virt[at, :] = jnp.dot(dense[at, :], gvm[...], preferred_element_type=jnp.float32).astype(jnp.bfloat16)
            return 0

        lax.fori_loop(0, 4, virt_step, 0, unroll=True)

        def occ_step(k, _):
            at = pl.ds(pl.multiple_of(k * 256, 256), 256)
            occ = jnp.dot(gop[at, :], virt[...], preferred_element_type=jnp.float32)
            for h in range(8):
                even, odd = occ[h * 32:h * 32 + 16], occ[h * 32 + 16:h * 32 + 32]
                even = jnp.concatenate([even[:, :128], even[:, 128:]], axis=0)
                odd = jnp.concatenate([odd[:, :128], odd[:, 128:]], axis=0)
                first = jnp.where(low16, even, pltpu.roll(odd, 64, 1)).astype(jnp.bfloat16)
                second = jnp.where(low16, pltpu.roll(even, 64, 1), odd).astype(jnp.bfloat16)
                lanes = pl.ds(pl.multiple_of(k * 1024 + h * 128, 128), 128)
                flat[pl.ds(pl.multiple_of(f * 64, 32), 32), lanes] = first
                flat[pl.ds(pl.multiple_of(f * 64 + 32, 32), 32), lanes] = second
            return 0

        lax.fori_loop(0, 4, occ_step, 0, unroll=True)

    row64 = lax.broadcasted_iota(jnp.int32, (64, 128), 0)
    want64 = (row64 % 16) * 16 + j * 4 + ((row64 % 32) // 16) * 2 + row64 // 32
    out_lane = lax.broadcasted_iota(jnp.int32, (8, 128), 1)

    def contract(o, p):
        other = jnp.concatenate([slabs[o, q, pl.ds(2 * p, 2)].reshape(32, 4096) for q in range(4)], axis=0)
        pick = idbuf[o] == want64.astype(jnp.float32)
        halves = jnp.zeros((8, 128), jnp.float32)
        for m in range(2):
            gram = lax.dot_general(flat[m * 256:(m + 1) * 256, :], other, NT, preferred_element_type=jnp.float32)
            for f in range(4):
                kept = jnp.sum(jnp.where(pick, gram[f * 64:(f + 1) * 64], 0.0), axis=0, keepdims=True)
                halves = jnp.where(lax.broadcasted_iota(jnp.int32, (8, 128), 0) == m * 4 + f, kept, halves)
        add = jnp.zeros((8, 128), jnp.float32)
        for q in range(2):
            total = jnp.sum(jnp.where((out_lane // 16) % 2 == q, halves, 0.0), axis=1, keepdims=True)
            add = add + jnp.where(out_lane == o * 8 + p * 2 + q, total, 0.0)
        part[...] += add

    def contract_wave(w):
        t, p = w // 4, w % 4
        for d in (0, 1):
            @pl.when(here(d, t))
            def _():
                contract(origin(d, t), p)

    arrive(2)
    spread(0)

    def first_phase(f, _):
        one_function(f)
        arrive(f + 3)
        spread(f + 1)
        return 0

    lax.fori_loop(0, 8, first_phase, 0)
    for step in range(1, nz):
        ids_copy(step).wait_send()
        remote(ids_n, idbuf.at[z], isend.at[step], irecv.at[step], right).wait_recv()

    def own_slab(p, _):
        contract(z, p)
        arrive(11 + p)
        spread(9 + p)
        return 0

    lax.fori_loop(0, 4, own_slab, 0)

    def second_phase(u, _):
        @pl.when(u + 15 < waves)
        def _():
            arrive(u + 15)

        @pl.when(u + 13 < waves)
        def _():
            spread(u + 13)
        collect(2 * u)
        collect(2 * u + 1)
        contract_wave(u)
        return 0

    lax.fori_loop(0, waves // 2, second_phase, 0)

    def p_copy(k, dev):
        return remote(part, parts.at[k], psend.at[k], precv.at[k], dev)

    for k, dev in enumerate((across, mate, diag)):
        p_copy(k, dev).start()

    def finish(w, _):
        t, p = w // pieces, w % pieces
        for d in (0, 1):
            @pl.when(here(d, t))
            def _():
                o = origin(d, t)

                @pl.when(passes(d, t))
                def _():
                    z_copy(d, w, o, p).wait_send()
                x_copy(d, w, o, p, j).wait_send()
                c_copy(d, w, 0, o, p, j).wait_send()
                c_copy(d, w, 1, o, p, jx).wait_send()
        return 0

    lax.fori_loop(0, waves, finish, 0)
    for p in range(pieces):
        @pl.when(z < nz - 1)
        def _():
            own(p, 0).wait_send()

        @pl.when(z > 0)
        def _():
            own(p, 1).wait_send()
    for k, dev in enumerate((across, mate, diag)):
        p_copy(k, dev).wait()
    total = part[...] + parts[0] + parts[1] + parts[2]
    wide = out.shape[1]
    result = jnp.zeros(out.shape, jnp.float32)
    for q in range(4):
        result = jnp.where(j == q, total[:, q * wide:(q + 1) * wide], result)
    out[...] = result


def fused(nz, ri_tensor, pair_ids, atom_size, green_occ, green_virt):
    waves = (nz - 1) * 8
    vmem = pl.BlockSpec(memory_space=pltpu.VMEM)
    bf16 = jnp.bfloat16
    dma = pltpu.SemaphoreType.DMA
    return pl.pallas_call(
        functools.partial(gather_kernel, nz),
        out_shape=jax.ShapeDtypeStruct((8, nz * 2), jnp.float32),
        in_specs=[pl.BlockSpec(memory_space=pl.ANY), vmem,
                  pl.BlockSpec(memory_space=pltpu.SMEM), vmem, vmem],
        out_specs=vmem,
        scratch_shapes=[
            pltpu.VMEM((nz, 4, 8, 16, 4096), bf16),
            pltpu.VMEM((1024, 1024), bf16),
            pltpu.VMEM((1024, 1024), bf16),
            pltpu.VMEM((1024, 1024), bf16),
            pltpu.VMEM((1024, 256), bf16),
            pltpu.VMEM((256, 64), bf16),
            pltpu.VMEM((1024, 1024), bf16),
            pltpu.VMEM((1024, 256), bf16),
            pltpu.VMEM((512, 4096), bf16),
            pltpu.VMEM((1, 128), jnp.float32),
            pltpu.VMEM((nz, 1, 128), jnp.float32),
            pltpu.VMEM((8, 128), jnp.float32),
            pltpu.VMEM((3, 8, 128), jnp.float32),
            dma((2, waves + 8)), dma((2, waves + 8)),
            dma((2, waves)), dma((2, waves)),
            dma((2, waves, 2)), dma((2, waves, 2)),
            dma((nz,)), dma((nz,)), dma((3,)), dma((3,)), dma((4,)),
        ],
        compiler_params=pltpu.CompilerParams(
            collective_id=0, has_side_effects=True, vmem_limit_bytes=56 * 1024 * 1024),
    )(ri_tensor, pair_ids.reshape(1, 64), atom_size, green_occ, green_virt)


def per_device(ri_tensor, pair_ids, atom_size, green_occ, green_virt):
    nz = lax.axis_size("tensor")
    split = (lax.axis_size("batch"), lax.axis_size("rep"))
    if nz == 4 and split == (2, 2) and ri_tensor.shape == (8, 64, 4096) and green_occ.shape == (1024, 1024):
        return fused(nz, ri_tensor, pair_ids, atom_size, green_occ, green_virt)
    return whole_blocks(ri_tensor, pair_ids, atom_size, green_occ, green_virt)


def whole_blocks(ri_tensor, pair_ids, atom_size, green_occ, green_virt):
    local_rows = ri_tensor.shape[0]
    slots = ri_tensor.shape[1]
    total_ao = green_occ.shape[0]
    columns = green_virt.shape[1]
    first_col = (lax.axis_index("batch") * lax.axis_size("rep") + lax.axis_index("rep")) * columns
    usable = (jnp.arange(BS)[None, :] < atom_size[:, None]).astype(jnp.bfloat16)
    row_atoms = pair_ids // NAT
    col_atoms = pair_ids % NAT
    blocks = ri_tensor.reshape(local_rows, slots, BS, BS)
    blocks = blocks * usable[row_atoms][None, :, :, None] * usable[col_atoms][None, :, None, :]
    selector_f = row_atoms[None, :] == jnp.arange(NAT)[:, None]
    selector = selector_f.astype(jnp.bfloat16)
    block_cols = col_atoms[:, None] * BS + jnp.arange(BS)[None, :]
    wanted = first_col + jnp.arange(columns)
    picker = (block_cols[:, :, None] == wanted[None, None, :]).astype(jnp.bfloat16)
    picked = jnp.einsum(
        "psij,sjk->psik", blocks, picker, preferred_element_type=jnp.float32
    ).astype(jnp.bfloat16)
    tensor_piece = jnp.einsum("as,psik->paik", selector, picked, preferred_element_type=jnp.float32)
    tensor_piece = tensor_piece.astype(jnp.bfloat16).reshape(local_rows, total_ao, columns)
    gv_blocks = green_virt.reshape(NAT, BS, columns)[col_atoms]
    per_slot = jnp.einsum("psij,sjk->psik", blocks, gv_blocks, preferred_element_type=jnp.float32)
    upper = per_slot.astype(jnp.bfloat16)
    rest = per_slot - upper.astype(jnp.float32)
    middle = rest.astype(jnp.bfloat16)
    lower = (rest - middle.astype(jnp.float32)).astype(jnp.bfloat16)
    virt_side = jnp.einsum("as,psik->paik", selector, upper, preferred_element_type=jnp.float32)
    virt_side = virt_side + jnp.einsum(
        "as,psik->paik", selector, middle, preferred_element_type=jnp.float32
    )
    virt_side = virt_side + jnp.einsum(
        "as,psik->paik", selector, lower, preferred_element_type=jnp.float32
    )
    virt_side = virt_side.astype(jnp.bfloat16).reshape(local_rows, total_ao, columns)
    occ_side = jnp.einsum(
        "lm,pms->pls", green_occ, virt_side, preferred_element_type=jnp.float32
    ).astype(jnp.bfloat16)
    moved_occ, moved_tensor = (
        lax.all_to_all(occ_side, "tensor", split_axis=1, concat_axis=0, tiled=True),
        lax.all_to_all(tensor_piece, "tensor", split_axis=1, concat_axis=0, tiled=True),
    )
    partial_value = jnp.einsum(
        "pls,qls->pq", moved_occ, moved_tensor, preferred_element_type=jnp.float32
    )
    own_rows = lax.psum_scatter(partial_value, "tensor", scatter_dimension=0, tiled=True)
    return lax.psum_scatter(own_rows, ("batch", "rep"), scatter_dimension=1, tiled=True)


def solution(mesh):
    in_specs = (
        P(("groups", "tensor"), None, None),
        P(("groups", "tensor")),
        P(),
        P(),
        P(None, ("batch", "rep")),
    )
    out_specs = P(("groups", "tensor"), ("batch", "rep"))
    return jax.shard_map(
        per_device, mesh=mesh, in_specs=in_specs, out_specs=out_specs, check_vma=False
    )
```

```python
import functools

import jax
import jax.numpy as jnp
from jax import lax
from jax.experimental import pallas as pl
from jax.experimental.pallas import tpu as pltpu
from jax.sharding import PartitionSpec as P

NAT = 16
BS = 64
MESH = pl.DeviceIdType.MESH
NT = (((1,), (1,)), ((), ()))


def gather_kernel(nz, ri, ids_k, size, go, gv, out,
                  slabs, perm, tmp, gop, gvm, sel, dense, virt, flat, ids_n, idbuf, part, parts,
                  zsend, zrecv, xsend, xrecv, csend, crecv, isend, irecv, psend, precv, lsem):
    z = lax.axis_index("tensor")
    b = lax.axis_index("batch")
    r = lax.axis_index("rep")
    j = b * 2 + r
    pieces = 8
    waves = (nz - 1) * pieces
    left = {"tensor": z - 1}
    right = {"tensor": z + 1}
    across = {"batch": 1 - b}
    mate = {"rep": 1 - r}
    diag = {"batch": 1 - b, "rep": 1 - r}

    barrier = pltpu.get_barrier_semaphore()
    for step in range(1, nz):
        pl.semaphore_signal(barrier, inc=1, device_id={"tensor": lax.rem(z + step, nz)}, device_id_type=MESH)
    for dev in (across, mate, diag):
        pl.semaphore_signal(barrier, inc=1, device_id=dev, device_id_type=MESH)

    def local(q):
        return pltpu.make_async_copy(
            ri.at[:, pl.ds(16 * q, 16), :],
            slabs.at[z, q], lsem.at[q])

    def remote(src, dst, s, d, dev):
        return pltpu.make_async_remote_copy(src_ref=src, dst_ref=dst, send_sem=s, recv_sem=d,
                                            device_id=dev, device_id_type=MESH)

    def spot(o, p, q):
        return slabs.at[o, q, pl.ds(p, 1)]

    for q in range(4):
        local(q).start()
    pl.semaphore_wait(barrier, nz - 1 + 3)

    def own(p, d):
        src = ri.at[pl.ds(p, 1), pl.ds(pl.multiple_of(16 * j, 16), 16), :]
        return remote(src, spot(z, p, j), zsend.at[d, p], zrecv.at[d, p], right if d == 0 else left)

    def ids_copy(step):
        dev = {"tensor": lax.rem(z + step, nz)}
        return remote(ids_n, idbuf.at[z], isend.at[step], irecv.at[step], dev)

    for p in range(pieces):
        @pl.when(z < nz - 1)
        def _():
            own(p, 0).start()

        @pl.when(z > 0)
        def _():
            own(p, 1).start()

    slot = lax.broadcasted_iota(jnp.int32, (64, 128), 0)
    spread_lane = lax.broadcasted_iota(jnp.int32, (64, 128), 1)
    chosen = jnp.where(slot == (spread_lane // 32) * 16 + spread_lane % 16, 1.0, 0.0).astype(jnp.bfloat16)
    listed = jnp.broadcast_to(ids_k[...], (8, 64)).astype(jnp.float32).astype(jnp.bfloat16)
    ids_n[...] = jnp.dot(listed, chosen, preferred_element_type=jnp.float32)[0:1]
    idbuf[z] = ids_n[...]
    for step in range(1, nz):
        ids_copy(step).start()

    def origin(d, t):
        return z - 1 - t if d == 0 else z + 1 + t

    def here(d, t):
        return t <= z - 1 if d == 0 else t <= nz - 2 - z

    def passes(d, t):
        ok = here(d, t)
        return jnp.logical_and(ok, z < nz - 1) if d == 0 else jnp.logical_and(ok, z > 0)

    def z_copy(d, w, o, p):
        return remote(spot(o, p, j), spot(o, p, j), zsend.at[d, w + pieces], zrecv.at[d, w + pieces],
                      right if d == 0 else left)

    def z_in(d, w, o, p):
        return remote(spot(o, p, j), spot(o, p, j), zsend.at[d, w], zrecv.at[d, w], right if d == 0 else left)

    def x_copy(d, w, o, p, q):
        return remote(spot(o, p, q), spot(o, p, q), xsend.at[d, w], xrecv.at[d, w], across)

    def c_copy(d, w, k, o, p, q):
        return remote(spot(o, p, q), spot(o, p, q), csend.at[d, w, k], crecv.at[d, w, k], mate)

    jx = (1 - b) * 2 + r
    jm = b * 2 + 1 - r
    jd = (1 - b) * 2 + 1 - r

    def arrive(w):
        t, p = w // pieces, w % pieces
        for d in (0, 1):
            @pl.when(here(d, t))
            def _():
                o = origin(d, t)
                z_in(d, w, o, p).wait_recv()
                x_copy(d, w, o, p, j).start()

                @pl.when(passes(d, t))
                def _():
                    z_copy(d, w, o, p).start()
                c_copy(d, w, 0, o, p, j).start()

    def spread(w):
        t, p = w // pieces, w % pieces
        for d in (0, 1):
            @pl.when(here(d, t))
            def _():
                o = origin(d, t)
                x_copy(d, w, o, p, jx).wait_recv()
                c_copy(d, w, 1, o, p, jx).start()

    def collect(w):
        t, p = w // pieces, w % pieces
        for d in (0, 1):
            @pl.when(here(d, t))
            def _():
                o = origin(d, t)
                c_copy(d, w, 0, o, p, jm).wait_recv()
                c_copy(d, w, 1, o, p, jd).wait_recv()

    lane = lax.broadcasted_iota(jnp.int32, (1, 1024), 1)
    limit = jnp.zeros((1, 1024), jnp.int32)
    for a in range(16):
        limit = jnp.where(lane // 64 == a, size[a], limit)

    def build(k, _):
        row = lax.broadcasted_iota(jnp.int32, (128, 1024), 0) + k * 128
        col = lax.broadcasted_iota(jnp.int32, (128, 1024), 1)
        place = (col % 64) * 16 + col // 64
        keep = jnp.logical_and(place == row, col % 64 < limit)
        perm[pl.ds(pl.multiple_of(k * 128, 128), 128), :] = jnp.where(keep, 1.0, 0.0).astype(jnp.bfloat16)
        return 0

    lax.fori_loop(0, 8, build, 0, unroll=True)

    def rows_in(k, _):
        at = pl.ds(pl.multiple_of(k * 256, 256), 256)
        tmp[at, :] = jnp.dot(perm[at, :], go[...], preferred_element_type=jnp.float32).astype(jnp.bfloat16)
        return 0

    lax.fori_loop(0, 4, rows_in, 0, unroll=True)
    arrive(0)

    def cols_in(k, _):
        at = pl.ds(pl.multiple_of(k * 256, 256), 256)
        gop[at, :] = lax.dot_general(tmp[at, :], perm[...], NT,
                                     preferred_element_type=jnp.float32).astype(jnp.bfloat16)
        return 0

    lax.fori_loop(0, 4, cols_in, 0, unroll=True)

    lane256 = lax.broadcasted_iota(jnp.int32, (64, 256), 1)
    sub256 = lax.broadcasted_iota(jnp.int32, (64, 256), 0)
    limit_c = jnp.zeros((64, 256), jnp.int32)
    for c in range(4):
        limit_c = jnp.where(lane256 // 64 == c, size[j * 4 + c], limit_c)
    for c in range(16):
        keep = jnp.logical_and(sub256 < size[c], lane256 % 64 < limit_c)
        block = gv[c * 64:(c + 1) * 64, :].astype(jnp.float32)
        gvm[c * 64:(c + 1) * 64, :] = jnp.where(keep, block, 0.0).astype(jnp.bfloat16)

    row = lax.broadcasted_iota(jnp.int32, (256, 64), 0)
    want = (row % 16) * 16 + ((row % 128) // 16) * 2 + row // 128
    sel[...] = jnp.where(ids_k[...] == want, 1.0, 0.0).astype(jnp.bfloat16)
    part[...] = jnp.zeros_like(part)
    for q in range(4):
        local(q).wait()

    low = lax.broadcasted_iota(jnp.int32, (128, 128), 1) < 64
    low16 = lax.broadcasted_iota(jnp.int32, (32, 128), 1) < 64

    def one_function(f):
        def unpack(k, _):
            at = pl.ds(pl.multiple_of(k * 256, 256), 256)
            mine = jnp.concatenate([slabs[z, q, f, :, at] for q in range(4)], axis=0)
            got = jnp.dot(sel[...], mine, preferred_element_type=jnp.float32)
            for h in range(2):
                even, odd = got[:128, h * 128:(h + 1) * 128], got[128:, h * 128:(h + 1) * 128]
                first = jnp.where(low, even, pltpu.roll(odd, 64, 1)).astype(jnp.bfloat16)
                second = jnp.where(low, pltpu.roll(even, 64, 1), odd).astype(jnp.bfloat16)
                base = k * 64 + h * 32
                for c in range(8):
                    dense[pl.ds(pl.multiple_of(base, 16), 16), c * 128:(c + 1) * 128] = first[c * 16:(c + 1) * 16]
                    dense[pl.ds(pl.multiple_of(base + 16, 16), 16), c * 128:(c + 1) * 128] = second[c * 16:(c + 1) * 16]
            return 0

        lax.fori_loop(0, 16, unpack, 0, unroll=True)

        def virt_step(k, _):
            at = pl.ds(pl.multiple_of(k * 256, 256), 256)
            virt[at, :] = jnp.dot(dense[at, :], gvm[...], preferred_element_type=jnp.float32).astype(jnp.bfloat16)
            return 0

        lax.fori_loop(0, 4, virt_step, 0, unroll=True)

        def occ_step(k, _):
            at = pl.ds(pl.multiple_of(k * 256, 256), 256)
            occ = jnp.dot(gop[at, :], virt[...], preferred_element_type=jnp.float32)
            for h in range(8):
                even, odd = occ[h * 32:h * 32 + 16], occ[h * 32 + 16:h * 32 + 32]
                even = jnp.concatenate([even[:, :128], even[:, 128:]], axis=0)
                odd = jnp.concatenate([odd[:, :128], odd[:, 128:]], axis=0)
                first = jnp.where(low16, even, pltpu.roll(odd, 64, 1)).astype(jnp.bfloat16)
                second = jnp.where(low16, pltpu.roll(even, 64, 1), odd).astype(jnp.bfloat16)
                lanes = pl.ds(pl.multiple_of(k * 1024 + h * 128, 128), 128)
                flat[pl.ds(pl.multiple_of(f * 64, 32), 32), lanes] = first
                flat[pl.ds(pl.multiple_of(f * 64 + 32, 32), 32), lanes] = second
            return 0

        lax.fori_loop(0, 4, occ_step, 0, unroll=True)

    row64 = lax.broadcasted_iota(jnp.int32, (64, 128), 0)
    want64 = (row64 % 16) * 16 + j * 4 + ((row64 % 32) // 16) * 2 + row64 // 32
    out_lane = lax.broadcasted_iota(jnp.int32, (8, 128), 1)

    def contract(o, p):
        other = jnp.concatenate([slabs[o, q, pl.ds(2 * p, 2)].reshape(32, 4096) for q in range(4)], axis=0)
        pick = idbuf[o] == want64.astype(jnp.float32)
        halves = jnp.zeros((8, 128), jnp.float32)
        for m in range(2):
            gram = lax.dot_general(flat[m * 256:(m + 1) * 256, :], other, NT, preferred_element_type=jnp.float32)
            for f in range(4):
                kept = jnp.sum(jnp.where(pick, gram[f * 64:(f + 1) * 64], 0.0), axis=0, keepdims=True)
                halves = jnp.where(lax.broadcasted_iota(jnp.int32, (8, 128), 0) == m * 4 + f, kept, halves)
        add = jnp.zeros((8, 128), jnp.float32)
        for q in range(2):
            total = jnp.sum(jnp.where((out_lane // 16) % 2 == q, halves, 0.0), axis=1, keepdims=True)
            add = add + jnp.where(out_lane == o * 8 + p * 2 + q, total, 0.0)
        part[...] += add

    def contract_wave(w):
        t, p = w // 4, w % 4
        for d in (0, 1):
            @pl.when(here(d, t))
            def _():
                contract(origin(d, t), p)

    arrive(1)

    def first_phase(f, _):
        one_function(f)
        arrive(f + 2)
        spread(f)
        return 0

    lax.fori_loop(0, 8, first_phase, 0)
    for step in range(1, nz):
        ids_copy(step).wait_send()
        remote(ids_n, idbuf.at[z], isend.at[step], irecv.at[step], right).wait_recv()

    def own_slab(p, _):
        contract(z, p)
        arrive(10 + p)
        spread(8 + p)
        return 0

    lax.fori_loop(0, 4, own_slab, 0)

    def second_phase(u, _):
        @pl.when(u + 14 < waves)
        def _():
            arrive(u + 14)
        spread(u + 12)
        collect(2 * u)
        collect(2 * u + 1)
        contract_wave(u)
        return 0

    lax.fori_loop(0, waves // 2, second_phase, 0)

    def p_copy(k, dev):
        return remote(part, parts.at[k], psend.at[k], precv.at[k], dev)

    for k, dev in enumerate((across, mate, diag)):
        p_copy(k, dev).start()

    def finish(w, _):
        t, p = w // pieces, w % pieces
        for d in (0, 1):
            @pl.when(here(d, t))
            def _():
                o = origin(d, t)

                @pl.when(passes(d, t))
                def _():
                    z_copy(d, w, o, p).wait_send()
                x_copy(d, w, o, p, j).wait_send()
                c_copy(d, w, 0, o, p, j).wait_send()
                c_copy(d, w, 1, o, p, jx).wait_send()
        return 0

    lax.fori_loop(0, waves, finish, 0)
    for p in range(pieces):
        @pl.when(z < nz - 1)
        def _():
            own(p, 0).wait_send()

        @pl.when(z > 0)
        def _():
            own(p, 1).wait_send()
    for k, dev in enumerate((across, mate, diag)):
        p_copy(k, dev).wait()
    total = part[...] + parts[0] + parts[1] + parts[2]
    wide = out.shape[1]
    result = jnp.zeros(out.shape, jnp.float32)
    for q in range(4):
        result = jnp.where(j == q, total[:, q * wide:(q + 1) * wide], result)
    out[...] = result


def fused(nz, ri_tensor, pair_ids, atom_size, green_occ, green_virt):
    waves = (nz - 1) * 8
    vmem = pl.BlockSpec(memory_space=pltpu.VMEM)
    bf16 = jnp.bfloat16
    dma = pltpu.SemaphoreType.DMA
    return pl.pallas_call(
        functools.partial(gather_kernel, nz),
        out_shape=jax.ShapeDtypeStruct((8, nz * 2), jnp.float32),
        in_specs=[pl.BlockSpec(memory_space=pl.ANY), vmem,
                  pl.BlockSpec(memory_space=pltpu.SMEM), vmem, vmem],
        out_specs=vmem,
        scratch_shapes=[
            pltpu.VMEM((nz, 4, 8, 16, 4096), bf16),
            pltpu.VMEM((1024, 1024), bf16),
            pltpu.VMEM((1024, 1024), bf16),
            pltpu.VMEM((1024, 1024), bf16),
            pltpu.VMEM((1024, 256), bf16),
            pltpu.VMEM((256, 64), bf16),
            pltpu.VMEM((1024, 1024), bf16),
            pltpu.VMEM((1024, 256), bf16),
            pltpu.VMEM((512, 4096), bf16),
            pltpu.VMEM((1, 128), jnp.float32),
            pltpu.VMEM((nz, 1, 128), jnp.float32),
            pltpu.VMEM((8, 128), jnp.float32),
            pltpu.VMEM((3, 8, 128), jnp.float32),
            dma((2, waves + 8)), dma((2, waves + 8)),
            dma((2, waves)), dma((2, waves)),
            dma((2, waves, 2)), dma((2, waves, 2)),
            dma((nz,)), dma((nz,)), dma((3,)), dma((3,)), dma((4,)),
        ],
        compiler_params=pltpu.CompilerParams(
            collective_id=0, has_side_effects=True, vmem_limit_bytes=56 * 1024 * 1024),
    )(ri_tensor, pair_ids.reshape(1, 64), atom_size, green_occ, green_virt)


def per_device(ri_tensor, pair_ids, atom_size, green_occ, green_virt):
    nz = lax.axis_size("tensor")
    split = (lax.axis_size("batch"), lax.axis_size("rep"))
    if nz == 4 and split == (2, 2) and ri_tensor.shape == (8, 64, 4096) and green_occ.shape == (1024, 1024):
        return fused(nz, ri_tensor, pair_ids, atom_size, green_occ, green_virt)
    return whole_blocks(ri_tensor, pair_ids, atom_size, green_occ, green_virt)


def whole_blocks(ri_tensor, pair_ids, atom_size, green_occ, green_virt):
    local_rows = ri_tensor.shape[0]
    slots = ri_tensor.shape[1]
    total_ao = green_occ.shape[0]
    columns = green_virt.shape[1]
    first_col = (lax.axis_index("batch") * lax.axis_size("rep") + lax.axis_index("rep")) * columns
    usable = (jnp.arange(BS)[None, :] < atom_size[:, None]).astype(jnp.bfloat16)
    row_atoms = pair_ids // NAT
    col_atoms = pair_ids % NAT
    blocks = ri_tensor.reshape(local_rows, slots, BS, BS)
    blocks = blocks * usable[row_atoms][None, :, :, None] * usable[col_atoms][None, :, None, :]
    selector_f = row_atoms[None, :] == jnp.arange(NAT)[:, None]
    selector = selector_f.astype(jnp.bfloat16)
    block_cols = col_atoms[:, None] * BS + jnp.arange(BS)[None, :]
    wanted = first_col + jnp.arange(columns)
    picker = (block_cols[:, :, None] == wanted[None, None, :]).astype(jnp.bfloat16)
    picked = jnp.einsum(
        "psij,sjk->psik", blocks, picker, preferred_element_type=jnp.float32
    ).astype(jnp.bfloat16)
    tensor_piece = jnp.einsum("as,psik->paik", selector, picked, preferred_element_type=jnp.float32)
    tensor_piece = tensor_piece.astype(jnp.bfloat16).reshape(local_rows, total_ao, columns)
    gv_blocks = green_virt.reshape(NAT, BS, columns)[col_atoms]
    per_slot = jnp.einsum("psij,sjk->psik", blocks, gv_blocks, preferred_element_type=jnp.float32)
    upper = per_slot.astype(jnp.bfloat16)
    rest = per_slot - upper.astype(jnp.float32)
    middle = rest.astype(jnp.bfloat16)
    lower = (rest - middle.astype(jnp.float32)).astype(jnp.bfloat16)
    virt_side = jnp.einsum("as,psik->paik", selector, upper, preferred_element_type=jnp.float32)
    virt_side = virt_side + jnp.einsum(
        "as,psik->paik", selector, middle, preferred_element_type=jnp.float32
    )
    virt_side = virt_side + jnp.einsum(
        "as,psik->paik", selector, lower, preferred_element_type=jnp.float32
    )
    virt_side = virt_side.astype(jnp.bfloat16).reshape(local_rows, total_ao, columns)
    occ_side = jnp.einsum(
        "lm,pms->pls", green_occ, virt_side, preferred_element_type=jnp.float32
    ).astype(jnp.bfloat16)
    moved_occ, moved_tensor = (
        lax.all_to_all(occ_side, "tensor", split_axis=1, concat_axis=0, tiled=True),
        lax.all_to_all(tensor_piece, "tensor", split_axis=1, concat_axis=0, tiled=True),
    )
    partial_value = jnp.einsum(
        "pls,qls->pq", moved_occ, moved_tensor, preferred_element_type=jnp.float32
    )
    own_rows = lax.psum_scatter(partial_value, "tensor", scatter_dimension=0, tiled=True)
    return lax.psum_scatter(own_rows, ("batch", "rep"), scatter_dimension=1, tiled=True)


def solution(mesh):
    in_specs = (
        P(("groups", "tensor"), None, None),
        P(("groups", "tensor")),
        P(),
        P(),
        P(None, ("batch", "rep")),
    )
    out_specs = P(("groups", "tensor"), ("batch", "rep"))
    return jax.shard_map(
        per_device, mesh=mesh, in_specs=in_specs, out_specs=out_specs, check_vma=False
    )
```
